256 devices in a mesh: dp: 8 (over z_lo, core), row: 4 (over x), col: 8 (over z_hi, y).
Axes of the slice: x: 4, y: 4, z: 8 (z_hi: 2, z_lo: 4; z = z_hi * 4 + z_lo), core: 2. Of those that a mesh axis runs over, the one named last changes fastest.
Arguments:
- inputs: bfloat16 [1024, 8192], P('dp', ('row', 'col')), may hold values from -6 to 6
- grad_out: bfloat16 [1024, 8192], P('dp', ('row', 'col')), may hold values from -6 to 6
- up_blocks: bfloat16 [4096, 128, 128], P(('row', 'col')), may hold values from -0.125 to 0.125
- up_index: int32 [4096], P(('row', 'col')), may hold values from 0 to 63, as said below
- down_blocks: bfloat16 [4096, 128, 128], P(('row', 'col')), may hold values from -0.0625 to 0.0625
- down_index: int32 [4096], P(('row', 'col')), may hold values from 0 to 255, as said below
Outputs:
- outputs: bfloat16 [1024, 8192], P('dp', ('row', 'col'))
- grad_in: bfloat16 [1024, 8192], P('dp', ('row', 'col'))
- grad_up: float32 [4096, 128, 128], P(('row', 'col'), 'dp')
- grad_down: float32 [4096, 128, 128], P(('row', 'col'), 'dp')
The draws below stay inside these ranges and needn't reach their ends.
Inputs may be any that keep to these rules, and one draw needn't show every extreme that they name: `up_index`: for each row tile r and column block j, the 4 entries of run (r, j) name distinct row blocks of row tile r. Within row tile r and column tile c they are r * 16 + ((j mod 16) XOR m XOR o), m over a set of 4 values closed under XOR, o fixed for the tile. `down_index`: for each row tile r, column tile c and feature block i of row tile r, the 8 entries name distinct hidden-unit blocks of column tile c: c * 32 + ((i mod 32) XOR m XOR o), m over a set of 8 values closed under XOR, o fixed for the tile.
All inputs are finite; a program needn't handle non-finite values.
Results may differ from the reference program's by a relative error of at most 0.024.
Values may be sent and summed in bfloat16 or wider, within the bound.
No kernel may reach another device: no remote copies, remote signals or barrier semaphores. Data moves between devices by JAX's collectives and lax.ppermute only.
A program may use at most 128 MiB of HBM per device.

```python
import jax
import jax.numpy as jnp
from jax import lax

D = 8192
FF = 32768
BS = 128
KB = 4
KB2 = 8
TOK_DEV = 128
TOKENS = 1024
UP_BLOCKS = 4096
DOWN_BLOCKS = 4096
N_DP = 8
N_ROW = 4
N_COL = 8


def draw_up_index(key, part):
    row_blocks = D // BS // N_ROW
    col_blocks = FF // BS // N_COL
    width_bits = row_blocks.bit_length() - 1
    key_first, key_step, key_shift = jax.random.split(jax.random.fold_in(key, 11), 3)
    bit_first = jax.random.randint(key_first, (N_ROW, N_COL, 1), 0, width_bits)
    bit_second = (bit_first + jax.random.randint(key_step, (N_ROW, N_COL, 1), 1, width_bits)) % width_bits
    members = jnp.arange(KB, dtype=jnp.int32)
    xor_masks = members % 2 * jnp.left_shift(jnp.int32(1), bit_first) + members // 2 * jnp.left_shift(jnp.int32(1), bit_second)
    shifts = jax.random.randint(key_shift, (N_ROW, N_COL, 1, 1), 0, row_blocks)
    shifts = shifts.at[0, 0, 0, 0].set(0)
    shifts = shifts.at[N_ROW - 1, 0, 0, 0].set(row_blocks - 1)
    within = (jnp.arange(col_blocks, dtype=jnp.int32) % row_blocks)[:, None]
    local_rows = jnp.bitwise_xor(jnp.bitwise_xor(within, xor_masks[:, :, None, :]), shifts)
    tile_base = jnp.arange(N_ROW, dtype=jnp.int32)[:, None, None, None] * row_blocks
    return (local_rows + tile_base).reshape(-1).astype(jnp.int32)


def draw_down_index(key, part):
    row_blocks = D // BS // N_ROW
    col_blocks = FF // BS // N_COL
    width_bits = col_blocks.bit_length() - 1
    key_rank, key_shift = jax.random.split(jax.random.fold_in(key, 23), 2)
    scores = jax.random.randint(key_rank, (N_ROW, N_COL, width_bits), 0, 1 << 20) * width_bits + jnp.arange(width_bits, dtype=jnp.int32)
    ordered = jnp.argsort(scores, axis=-1).astype(jnp.int32)
    members = jnp.arange(KB2, dtype=jnp.int32)
    xor_masks = jnp.zeros((N_ROW, N_COL, KB2), jnp.int32)
    for position in range(3):
        digit = members // 2 ** position % 2
        xor_masks = xor_masks + digit * jnp.left_shift(jnp.int32(1), ordered[:, :, position:position + 1])
    shifts = jax.random.randint(key_shift, (N_ROW, N_COL, 1, 1), 0, col_blocks)
    shifts = shifts.at[0, 0, 0, 0].set(0)
    shifts = shifts.at[0, N_COL - 1, 0, 0].set(col_blocks - 1)
    within = (jnp.arange(row_blocks, dtype=jnp.int32) % col_blocks)[:, None]
    local_cols = jnp.bitwise_xor(jnp.bitwise_xor(within, xor_masks[:, :, None, :]), shifts)
    tile_base = jnp.arange(N_COL, dtype=jnp.int32)[None, :, None, None] * col_blocks
    return (local_cols + tile_base).reshape(-1).astype(jnp.int32)


def block_levels(stream_key, dims, pieces, smallest, high):
    level, own = 1.0, jax.random.fold_in(stream_key, 6)
    for dim, parts in pieces:
        draws = jnp.exp(jax.random.uniform(jax.random.fold_in(own, dim), (parts,), jnp.float32, smallest / len(pieces), high / len(pieces)))
        level = level * jnp.repeat(draws, dims[dim] // parts).reshape([-1 if axis == dim else 1 for axis in range(len(dims))])
    return level


def noise(key, extent, scale, reach, cuts=(), kind=jnp.bfloat16):
    values = jax.random.normal(key, extent, jnp.float32) * scale
    if len(cuts) > 0:
        values = block_levels(key, extent, cuts, -0.22, 0.18) * values
    return jnp.clip(values, min=-reach, max=reach).astype(kind)


def setup_inputs(seed: int = 0) -> dict:
    seeds = jax.random.split(jax.random.key(seed), 7)
    return {
        "inputs": noise(seeds[0], (TOKENS, D), 1.0, 6.0, ((0, 8), (1, 32))),
        "grad_out": noise(seeds[1], (TOKENS, D), 1.0, 6.0, ((0, 8), (1, 32))),
        "up_blocks": noise(seeds[2], (UP_BLOCKS, BS, BS), (KB * N_ROW * BS) ** -0.5, 0.125, ((0, 32),)),
        "up_index": draw_up_index(jax.random.fold_in(seeds[6], 71), 0),
        "down_blocks": noise(seeds[4], (DOWN_BLOCKS, BS, BS), (KB2 * N_COL * BS) ** -0.5, 0.0625, ((0, 32),)),
        "down_index": draw_down_index(jax.random.fold_in(seeds[6], 71), 0),
    }


gelu_scale = 0.7978845608028654
cubic_term = 0.044715


def gelu_value(values):
    inside = gelu_scale * (values + cubic_term * values * values * values)
    return 0.5 * values * (1.0 + jnp.tanh(inside))


def gelu_slope(values):
    tangent = jnp.tanh(gelu_scale * (values + cubic_term * values * values * values))
    return 0.5 * (1.0 + tangent) + 0.5 * values * (1.0 - tangent * tangent) * gelu_scale * (1.0 + 3.0 * cubic_term * values * values)


def rounded(values):
    return lax.optimization_barrier(values.astype(jnp.bfloat16)).astype(jnp.float32)


def reference(inputs, grad_out, up_blocks, up_index, down_blocks, down_index):
    row_blocks = D // BS // N_ROW
    col_blocks = FF // BS // N_COL
    up_tiles = up_blocks.astype(jnp.float32).reshape(N_ROW, FF // BS, KB, BS, BS)
    up_where = up_index.astype(jnp.int32).reshape(N_ROW, FF // BS, KB)
    down_block_tiles = down_blocks.astype(jnp.float32).reshape(N_ROW, N_COL, row_blocks, KB2, BS, BS)
    down_where = down_index.astype(jnp.int32).reshape(N_ROW, N_COL, row_blocks, KB2)
    row_ids = jnp.arange(N_ROW, dtype=jnp.int32)[:, None]
    col_ids = jnp.arange(N_COL, dtype=jnp.int32)[:, None]

    def one_group(totals, slices):
        x_group, g_group = slices
        x_pieces = x_group.astype(jnp.float32).reshape(TOK_DEV, D // BS, BS)
        g_tiles = g_group.astype(jnp.float32).reshape(TOK_DEV, N_ROW, row_blocks, BS)
        partial_block_value = jnp.zeros((TOK_DEV, N_ROW, FF // BS, BS), jnp.float32)
        for group_member in range(KB):
            picked = jnp.take(x_pieces, up_where[:, :, group_member], axis=1)
            partial_block_value = partial_block_value + jnp.einsum("nrjd,rjde->nrje", picked, up_tiles[:, :, group_member])
        hidden = jnp.sum(rounded(partial_block_value), axis=1)
        active = gelu_value(hidden).astype(jnp.bfloat16)
        act_float = active.astype(jnp.float32)
        out_partial = jnp.zeros((TOK_DEV, N_COL, N_ROW, row_blocks, BS), jnp.float32)
        for group_member in range(KB2):
            picked = jnp.take(act_float, down_where[..., group_member], axis=1)
            out_partial = out_partial + jnp.einsum("nrcid,rcide->ncrie", picked, down_block_tiles[:, :, :, group_member])
        outputs = jnp.sum(rounded(out_partial), axis=1).reshape(TOK_DEV, D).astype(jnp.bfloat16)
        back_partial = jnp.zeros((TOK_DEV, N_ROW, FF // BS, BS), jnp.float32)
        for group_member in range(KB2):
            contrib = jnp.einsum("nrie,rcide->nrcid", g_tiles, down_block_tiles[:, :, :, group_member])
            targets = down_where[..., group_member].reshape(N_ROW, N_COL * row_blocks)
            back_partial = back_partial.at[:, row_ids, targets].add(contrib.reshape(TOK_DEV, N_ROW, N_COL * row_blocks, BS))
        grad_act = jnp.sum(rounded(back_partial), axis=1)
        grad_hidden = (grad_act * gelu_slope(hidden)).astype(jnp.bfloat16)
        hidden_float = grad_hidden.astype(jnp.float32)
        hidden_block_tiles = hidden_float.reshape(TOK_DEV, N_COL, col_blocks, BS)
        up_by_col = up_tiles.reshape(N_ROW, N_COL, col_blocks, KB, BS, BS)
        where_by_col = up_where.reshape(N_ROW, N_COL, col_blocks, KB)
        in_partial = jnp.zeros((TOK_DEV, N_COL, D // BS, BS), jnp.float32)
        for group_member in range(KB):
            contrib = jnp.einsum("ncje,rcjde->ncrjd", hidden_block_tiles, up_by_col[:, :, :, group_member])
            targets = jnp.transpose(where_by_col[..., group_member], (1, 0, 2)).reshape(N_COL, N_ROW * col_blocks)
            in_partial = in_partial.at[:, col_ids, targets].add(contrib.reshape(TOK_DEV, N_COL, N_ROW * col_blocks, BS))
        grad_in = jnp.sum(rounded(in_partial), axis=1).reshape(TOK_DEV, D).astype(jnp.bfloat16)
        up_grads = []
        for group_member in range(KB):
            picked = jnp.take(x_pieces, up_where[:, :, group_member], axis=1)
            up_grads.append(jnp.einsum("nrjd,nje->rjde", picked, hidden_float))
        up_block_group = jnp.stack(up_grads, axis=2).reshape(-1, BS, BS)
        down_grads = []
        for group_member in range(KB2):
            picked = jnp.take(act_float, down_where[..., group_member], axis=1)
            down_grads.append(jnp.einsum("nrcid,nrie->rcide", picked, g_tiles))
        down_group = jnp.stack(down_grads, axis=3).reshape(-1, BS, BS)
        totals = (totals[0] + rounded(up_block_group), totals[1] + rounded(down_group))
        return totals, (outputs, grad_in)

    start_totals = (jnp.zeros((N_ROW * (FF // BS) * KB, BS, BS), jnp.float32),
                    jnp.zeros((N_ROW * N_COL * row_blocks * KB2, BS, BS), jnp.float32))
    slices = (inputs.reshape(N_DP, TOK_DEV, D), grad_out.reshape(N_DP, TOK_DEV, D))
    totals, stacked = lax.scan(one_group, start_totals, slices)
    outputs = stacked[0].reshape(N_DP * TOK_DEV, D)
    grad_in = stacked[1].reshape(N_DP * TOK_DEV, D)
    return (outputs, grad_in, totals[0], totals[1])
```

```python
import jax
import jax.numpy as jnp
from jax import lax
from jax.experimental import pallas as pl
from jax.experimental.pallas import tpu as pltpu
from jax.sharding import Mesh
from jax.sharding import PartitionSpec as P

KB = 4
KB2 = 8
BS = 128
ROWS = 16
COLS = 32

gelu_scale = 0.7978845608028654
cubic_term = 0.044715


def gelu_value(values):
    inside = gelu_scale * (values + cubic_term * values * values * values)
    return 0.5 * values * (1.0 + jnp.tanh(inside))


def gelu_slope(values):
    tangent = jnp.tanh(gelu_scale * (values + cubic_term * values * values * values))
    return 0.5 * (1.0 + tangent) + 0.5 * values * (1.0 - tangent * tangent) * gelu_scale * (
        1.0 + 3.0 * cubic_term * values * values
    )


SMEM = pl.BlockSpec(memory_space=pltpu.SMEM)
VMEM = pl.BlockSpec(memory_space=pltpu.VMEM)
BF = jnp.bfloat16
F32 = jnp.float32


def call(kernel, scalars, arrays, outs, scratch=(), flops=1.1e9, name=None):
    moved = sum(a.size * a.dtype.itemsize for a in arrays)
    return pl.pallas_call(
        kernel,
        out_shape=outs,
        in_specs=[SMEM] * len(scalars) + [VMEM] * len(arrays),
        out_specs=[VMEM] * len(outs),
        scratch_shapes=list(scratch),
        compiler_params=pltpu.CompilerParams(vmem_limit_bytes=28 * 2**20),
        cost_estimate=pl.CostEstimate(flops=int(flops), bytes_accessed=int(moved), transcendentals=0),
        name=name,
    )(*scalars, *arrays)


def up_kernel(order, where, x, w, *outs):
    for slot, out in enumerate(outs):

        def step(jj, carry):
            j = order[slot * 8 + jj]
            lhs = jnp.concatenate([x[where[j * KB + k]] for k in range(KB)], axis=1)
            rhs = w[pl.ds(j * KB, KB)].reshape(KB * BS, BS)
            out[jj] = jnp.dot(lhs, rhs, preferred_element_type=F32).astype(BF)
            return carry

        lax.fori_loop(0, 8, step, 0, unroll=4)


def down_kernel(order, where, a, w, *outs):
    for slot, out in enumerate(outs):

        def step(ii, carry):
            i = order[slot * 4 + ii]
            lhs = jnp.concatenate([a[where[i * KB2 + k]] for k in range(KB2)], axis=1)
            rhs = w[pl.ds(i * KB2, KB2)].reshape(KB2 * BS, BS)
            out[ii] = jnp.dot(lhs, rhs, preferred_element_type=F32).astype(BF)
            return carry

        lax.fori_loop(0, 4, step, 0, unroll=2)


def spread_kernel(runs, width, pieces, order, where, v, w, *rest):
    outs, acc = rest[:-1], rest[-1]
    acc[...] = jnp.zeros_like(acc)

    def step(loc, carry):
        run = order[loc]
        rhs = w[pl.ds(run * width, width)].reshape(width * BS, BS)
        got = lax.dot_general(v[loc], rhs, (((1,), (1,)), ((), ())), preferred_element_type=F32)
        for k in range(width):
            at = where[run * width + k]
            acc[at] = acc[at] + got[:, k * BS:(k + 1) * BS]
        return carry

    lax.fori_loop(0, runs, step, 0, unroll=2)
    for slot, out in enumerate(outs):
        out[...] = acc[slot * pieces:(slot + 1) * pieces].astype(BF)


def term_kernel(runs, width, many, spot, where, place, u0, u1, v0, v1, out, turned):
    half = place[0]

    def turn(b, carry):
        turned[b, :, :BS] = u0[b].T
        turned[b, :, BS:] = u1[b].T
        return carry

    lax.fori_loop(0, many, turn, 0, unroll=4)

    def step(n, carry):
        run = half * runs + n
        lhs = jnp.concatenate([turned[where[run * width + k]] for k in range(width)], axis=0)
        at = spot[run]
        rhs = jnp.concatenate([v0[at], v1[at]], axis=0)
        got = jnp.dot(lhs, rhs, preferred_element_type=F32).astype(BF)
        got = got.reshape(width, 4, 2, 16, BS)
        for z in range(4):
            for side in range(2):
                out[z, jnp.bitwise_xor(side, half), pl.ds(n * width, width)] = got[:, z, side]
        return carry

    lax.fori_loop(0, runs, step, 0, unroll=2)


def shift(value, axis, size, by):
    return lax.ppermute(value, axis, [(i, (i + by) % size) for i in range(size)])


def swap(value, axis):
    return lax.ppermute(value, axis, [(0, 1), (1, 0)])


def spread(own, axis):
    return jnp.concatenate([own] + [shift(own, axis, 4, -s) for s in (1, 2, 3)], axis=0)


def total(parts, axis):
    got = [shift(parts[s], axis, 4, s) for s in (1, 2, 3)]
    return sum((g.astype(F32) for g in got), parts[0].astype(F32))


def gather_features(value):
    pieces = jnp.transpose(value.reshape(BS, 2, BS), (1, 0, 2))
    return spread(jnp.concatenate([pieces, swap(pieces, "h")], axis=0), "y")


def scatter_features(parts):
    mine = total(parts, "y").reshape(2, 2, BS, BS)
    done = mine[0] + swap(mine[1].astype(BF), "h").astype(F32)
    return jnp.transpose(done.astype(BF), (1, 0, 2)).reshape(BS, 2 * BS)


def finish(terms, half):
    mine = lax.psum_scatter(terms, "z", scatter_dimension=0, tiled=True)[0]
    own, other = mine[0], swap(mine[1], "q")
    low = jnp.where(half == 0, own, other)
    high = jnp.where(half == 0, other, own)
    return jnp.concatenate([low, high], axis=0).astype(F32)


def local(inputs, grad_out, up_blocks, up_index, down_blocks, down_index):
    r, h, y, q = (lax.axis_index(a) for a in ("row", "h", "y", "q"))
    half = q.reshape(1).astype(jnp.int32)
    c = h * 4 + y

    def feature_spot(b):
        return ((b // 2 % 4 - y) % 4) * 4 + jnp.bitwise_xor(b // 8, h) * 2 + b % 2

    def feature_at(s):
        return jnp.bitwise_xor(s // 2 % 2, h) * 8 + ((s // 4 + y) % 4) * 2 + s % 2

    def hidden_spot(f):
        return ((f // 8 - r) % 4) * 8 + f % 8

    def hidden_at(s):
        return ((s // 8 + r) % 4) * 8 + s % 8

    features, units = jnp.arange(ROWS, dtype=jnp.int32), jnp.arange(COLS, dtype=jnp.int32)
    up_where = feature_spot(up_index - r * ROWS)
    down_where = hidden_spot(down_index - c * COLS)
    feature_spots, feature_order = feature_spot(features), feature_at(features)
    hidden_spots, hidden_order = hidden_spot(units), hidden_at(units)

    x = gather_features(inputs)
    g = gather_features(grad_out)
    piece = jax.ShapeDtypeStruct((8, BS, BS), BF)
    slab = jax.ShapeDtypeStruct((4, BS, BS), BF)

    up = call(up_kernel, (hidden_order, up_where), (x, up_blocks), [piece] * 4, name="up")
    hidden = total(up, "row")
    active = spread(gelu_value(hidden).astype(BF), "row")

    back = call(
        lambda *a: spread_kernel(ROWS, KB2, 8, *a), (feature_order, down_where), (g, down_blocks), [piece] * 4,
        [pltpu.VMEM((COLS, BS, BS), F32)], name="back",
    )
    grad_hidden = spread((total(back, "row") * gelu_slope(hidden)).astype(BF), "row")

    x2, g2 = swap(x, "q"), swap(g, "q")
    terms = jax.ShapeDtypeStruct((4, 2, 64, 16, BS), BF)

    (down_terms,) = call(
        lambda *a: term_kernel(8, KB2, COLS, *a), (feature_spots, down_where, half),
        (active, swap(active, "q"), g, g2), [terms], [pltpu.VMEM((COLS, BS, 2 * BS), BF)], name="down_terms",
    )
    grad_down = finish(down_terms, q)
    (up_terms,) = call(
        lambda *a: term_kernel(16, KB, ROWS, *a), (hidden_spots, up_where, half),
        (x, x2, grad_hidden, swap(grad_hidden, "q")), [terms], [pltpu.VMEM((ROWS, BS, 2 * BS), BF)], name="up_terms",
    )
    grad_up = finish(up_terms, q)

    down = call(down_kernel, (feature_order, down_where), (active, down_blocks), [slab] * 4, name="down")
    outputs = scatter_features(down)
    into = call(
        lambda *a: spread_kernel(COLS, KB, 4, *a), (hidden_order, up_where), (grad_hidden, up_blocks), [slab] * 4,
        [pltpu.VMEM((ROWS, BS, BS), F32)], name="into",
    )
    grad_in = scatter_features(into)
    return outputs, grad_in, grad_up, grad_down


def solution(mesh):
    fine = Mesh(mesh.devices.reshape(4, 2, 4, 2, 4), ("z", "q", "row", "h", "y"))
    tokens, width = ("z", "q"), ("row", "h", "y")
    placed = (
        P(tokens, width),
        P(tokens, width),
        P(width, None, None),
        P(width),
        P(width, None, None),
        P(width),
    )
    return jax.shard_map(
        local,
        mesh=fine,
        in_specs=placed,
        out_specs=(P(tokens, width), P(tokens, width), P(width, tokens, None), P(width, tokens, None)),
        check_vma=False,
    )
```

```python
import jax
import jax.numpy as jnp
from jax import lax
from jax.experimental import pallas as pl
from jax.experimental.pallas import tpu as pltpu
from jax.sharding import Mesh
from jax.sharding import PartitionSpec as P

KB = 4
KB2 = 8
BS = 128
ROWS = 16
COLS = 32
BF = jnp.bfloat16
F32 = jnp.float32

gelu_scale = 0.7978845608028654
cubic_term = 0.044715


def gelu_both(values):
    tangent = jnp.tanh(gelu_scale * (values + cubic_term * values * values * values))
    value = 0.5 * values * (1.0 + tangent)
    slope = 0.5 * (1.0 + tangent) + 0.5 * values * (1.0 - tangent * tangent) * gelu_scale * (
        1.0 + 3.0 * cubic_term * values * values
    )
    return value, slope


SMEM = pl.BlockSpec(memory_space=pltpu.SMEM)
VMEM = pl.BlockSpec(memory_space=pltpu.VMEM)


def call(kernel, scalars, arrays, outs, scratch=(), flops=1.1e9, name=None):
    moved = sum(a.size * a.dtype.itemsize for a in arrays)
    return pl.pallas_call(
        kernel,
        out_shape=outs,
        in_specs=[SMEM] * len(scalars) + [VMEM] * len(arrays),
        out_specs=[VMEM] * len(outs),
        scratch_shapes=list(scratch),
        compiler_params=pltpu.CompilerParams(vmem_limit_bytes=28 * 2**20),
        cost_estimate=pl.CostEstimate(flops=int(flops), bytes_accessed=int(moved), transcendentals=0),
        name=name,
    )(*scalars, *arrays)


def lanes(half):
    return pl.ds(pl.multiple_of(half * BS, BS), BS)


def block(ref, at):
    return ref[at // 2, :, lanes(at % 2)]


def up_kernel(order, where, x, w, *outs):
    for slot, out in enumerate(outs):

        def step(jj, carry):
            j = order[slot * 8 + jj]
            lhs = jnp.concatenate([block(x, where[j * KB + k]) for k in range(KB)], axis=1)
            rhs = w[pl.ds(j * KB, KB)].reshape(KB * BS, BS)
            out[jj] = jnp.dot(lhs, rhs, preferred_element_type=F32).astype(BF)
            return carry

        lax.fori_loop(0, 8, step, 0, unroll=4)


def add_back(acc, run, where, width, rows, w):
    rhs = w[pl.ds(run * width, width)].reshape(width * BS, BS)
    got = lax.dot_general(rows, rhs, (((1,), (1,)), ((), ())), preferred_element_type=F32)
    for k in range(width):
        at = where[run * width + k]
        acc[at] = acc[at] + got[:, k * BS:(k + 1) * BS]


def back_kernel(order, where, g, w, *rest):
    outs, acc = rest[:-1], rest[-1]
    acc[...] = jnp.zeros_like(acc)

    def step(at, carry):
        add_back(acc, order[at], where, KB2, block(g, at), w)
        return carry

    lax.fori_loop(0, ROWS, step, 0, unroll=2)
    for o, out in enumerate(outs):
        out[...] = acc[o * 4:(o + 1) * 4].astype(BF)


def act_kernel(place, p0, p1, p2, p3, active, slope, own, other, turned):
    z, q = place[0], place[1]

    def step(b, carry):
        hidden = p0[b].astype(F32) + p1[b].astype(F32) + p2[b].astype(F32) + p3[b].astype(F32)
        value, slopes = gelu_both(hidden)
        slope[b] = slopes
        value = value.astype(BF)
        active[b] = value
        rows = value.T.reshape(4, 2, 16, BS)
        for zz in range(4):
            at = jnp.bitwise_and(zz - z + 4, 3)
            for side in range(2):
                turned[jnp.bitwise_xor(side, q), at, b] = rows[zz, side]
        return carry

    lax.fori_loop(0, 8, step, 0, unroll=2)
    own[...] = turned[0]
    other[...] = turned[1]


def turn_kernel(place, x, x2, out):
    z, q = place[0], place[1]

    def step(p, carry):
        for half in range(2):
            for group, ref in enumerate((x, x2)):
                rows = ref[p, :, half * BS:(half + 1) * BS].T.reshape(4, 2, 16, BS)
                for zz in range(4):
                    mine = jnp.where(q == 0, rows[zz, 0], rows[zz, 1])
                    out[p * 2 + half, jnp.bitwise_and(zz - z + 4, 3), :, group * BS:(group + 1) * BS] = mine
        return carry

    lax.fori_loop(0, 8, step, 0, unroll=2)


def up_terms_kernel(chunk, place, where, xt, v0, v1, *outs):
    r = place[2]

    def step(n, carry):
        row, jj = n // 4, n % 4
        j = row * 8 + chunk * 4 + jj
        at = jnp.bitwise_and(row - r + 4, 3) * 4 + jj
        lhs = jnp.concatenate([xt[where[j * KB + k]].reshape(64, 2 * BS) for k in range(KB)], axis=0)
        rhs = jnp.concatenate([v0[at], v1[at]], axis=0)
        got = jnp.dot(lhs, rhs, preferred_element_type=F32).astype(BF).reshape(KB, 4, 16, BS)
        for s, out in enumerate(outs):
            out[pl.ds(n * KB, KB)] = got[:, s]
        return carry

    lax.fori_loop(0, 16, step, 0, unroll=2)


def down_terms_kernel(spot, where, a, g0, g1, f0, f1, out):
    def step(i, carry):
        at = spot[i]
        runs = [where[i * KB2 + k] for k in range(KB2)]
        lhs, rhs = [], []
        for tq, (g, f) in enumerate(((g0, f0), (g1, f1))):
            for tz in range(4):
                lhs.append(jnp.concatenate([a[u // 8, tz, tq, u % 8] for u in runs], axis=0))
                rhs.append(block(g, at) if tz == 0 else f[at // 4, tz - 1, at // 2 % 2, :, lanes(at % 2)])
        got = jnp.dot(jnp.concatenate(lhs, axis=1), jnp.concatenate(rhs, axis=0), preferred_element_type=F32)
        out[pl.ds(i * KB2, KB2)] = got.reshape(KB2, 16, BS)
        return carry

    lax.fori_loop(0, ROWS, step, 0, unroll=2)


def down_kernel(order, where, a, w, *outs):
    for slot, out in enumerate(outs):
        for t in range(2):
            for half in range(2):
                i = order[slot * 4 + t * 2 + half]
                lhs = jnp.concatenate([a[where[i * KB2 + k]] for k in range(KB2)], axis=1)
                rhs = w[pl.ds(i * KB2, KB2)].reshape(KB2 * BS, BS)
                out[t, :, half * BS:(half + 1) * BS] = jnp.dot(lhs, rhs, preferred_element_type=F32).astype(BF)


def into_kernel(order, where, v0, v1, w, *rest):
    outs, acc = rest[:-1], rest[-1]
    acc[...] = jnp.zeros_like(acc)
    for chunk, v in enumerate((v0, v1)):

        def step(at, carry):
            add_back(acc, order[at // 4 * 8 + chunk * 4 + at % 4], where, KB, v[at], w)
            return carry

        lax.fori_loop(0, 16, step, 0, unroll=4)
    for slot, out in enumerate(outs):
        for t in range(2):
            for half in range(2):
                out[t, :, half * BS:(half + 1) * BS] = acc[slot * 4 + t * 2 + half].astype(BF)


def shift(value, axis, size, by):
    return lax.ppermute(value, axis, [(i, (i + by) % size) for i in range(size)])


def swap(value, axis):
    return lax.ppermute(value, axis, [(0, 1), (1, 0)])


def spread(own, axis):
    return jnp.concatenate([own] + [shift(own, axis, 4, -s) for s in (1, 2, 3)], axis=0)


def exchange(parts, axis):
    return [parts[0]] + [shift(parts[s], axis, 4, s) for s in (1, 2, 3)]


def total(parts):
    return sum((p.astype(F32) for p in parts[1:]), parts[0].astype(F32))


def scatter_features(parts):
    mine = total(exchange(parts, "y"))
    return (mine[0] + swap(mine[1].astype(BF), "h").astype(F32)).astype(BF)


def local(inputs, grad_out, up_blocks, up_index, down_blocks, down_index):
    z, q, r, h, y = (lax.axis_index(a).astype(jnp.int32) for a in ("z", "q", "row", "h", "y"))
    place = jnp.stack([z, q, r])
    c = h * 4 + y

    def feature_spot(b):
        return ((b // 2 % 4 - y) % 4) * 4 + jnp.bitwise_xor(b // 8, h) * 2 + b % 2

    def feature_at(s):
        return jnp.bitwise_xor(s // 2 % 2, h) * 8 + ((s // 4 + y) % 4) * 2 + s % 2

    def hidden_spot(f):
        return ((f // 8 - r) % 4) * 8 + f % 8

    def hidden_at(s):
        return ((s // 8 + r) % 4) * 8 + s % 8

    features, units = jnp.arange(ROWS, dtype=jnp.int32), jnp.arange(COLS, dtype=jnp.int32)
    up_where = feature_spot(up_index - r * ROWS)
    down_where = hidden_spot(down_index - c * COLS)
    feature_spots, feature_order = feature_spot(features), feature_at(features)
    hidden_order = hidden_at(units)

    def shape(*dims, dtype=BF):
        return jax.ShapeDtypeStruct(dims, dtype)

    x_own = jnp.stack([inputs, swap(inputs, "h")])
    g_own = jnp.stack([grad_out, swap(grad_out, "h")])
    x, g = spread(x_own, "y"), spread(g_own, "y")

    up = call(up_kernel, (hidden_order, up_where), (x, up_blocks), [shape(8, BS, BS)] * 4, name="up")
    back = call(
        back_kernel, (feature_order, down_where), (g, down_blocks), [shape(4, BS, BS)] * 8,
        [pltpu.VMEM((COLS, BS, BS), F32)], name="back",
    )
    active_own, slope, rows_own, rows_other = call(
        act_kernel, (place,), exchange(up, "row"),
        [shape(8, BS, BS), shape(8, BS, BS, dtype=F32)] + [shape(4, 8, 16, BS)] * 2,
        [pltpu.VMEM((2, 4, 8, 16, BS), BF)], flops=1e7, name="act",
    )
    (turned,) = call(turn_kernel, (place,), (x, swap(x, "q")), [shape(ROWS, 4, 16, 2 * BS)], flops=1e7, name="turn")

    grads, sums = [], []
    for chunk in range(2):
        own = (total(exchange(back[chunk::2], "row")) * slope[chunk * 4:chunk * 4 + 4]).astype(BF)
        grads.append(spread(own, "row"))
        terms = call(
            lambda *a: up_terms_kernel(chunk, *a), (place, up_where), (turned, grads[chunk], swap(grads[chunk], "q")),
            [shape(64, 16, BS)] * 4, flops=5e8, name="up_terms",
        )
        sums.append(total(exchange(terms, "z")).reshape(4, 1, 16, 16, BS))
    grad_up = jnp.concatenate(sums, axis=1).reshape(128, 16, BS)

    into = call(
        into_kernel, (hidden_order, up_where), (grads[0], grads[1], up_blocks), [shape(2, BS, 2 * BS)] * 4,
        [pltpu.VMEM((ROWS, BS, BS), F32)], name="into",
    )
    grad_in = scatter_features(into)

    active = spread(active_own, "row")
    down = call(down_kernel, (feature_order, down_where), (active, down_blocks), [shape(2, BS, 2 * BS)] * 4, name="down")
    outputs = scatter_features(down)

    rows_peer = swap(rows_other, "q")
    rows = exchange([jnp.stack([rows_own[s], rows_peer[s]]) for s in range(4)], "z")
    rows = spread(jnp.stack(rows)[None], "row")
    far = jnp.stack([shift(g_own, "z", 4, s) for s in (1, 2, 3)])
    far = spread(far[None], "y")
    (grad_down,) = call(
        down_terms_kernel, (feature_spots, down_where), (rows, g, swap(g, "q"), far, swap(far, "q")),
        [shape(128, 16, BS, dtype=F32)], name="down_terms",
    )
    return outputs, grad_in, grad_up, grad_down


def solution(mesh):
    fine = Mesh(mesh.devices.reshape(4, 2, 4, 2, 4), ("z", "q", "row", "h", "y"))
    tokens, width = ("z", "q"), ("row", "h", "y")
    placed = (
        P(tokens, width),
        P(tokens, width),
        P(width, None, None),
        P(width),
        P(width, None, None),
        P(width),
    )
    return jax.shard_map(
        local,
        mesh=fine,
        in_specs=placed,
        out_specs=(P(tokens, width), P(tokens, width), P(width, tokens, None), P(width, tokens, None)),
        check_vma=False,
    )
```

```python
import jax
import jax.numpy as jnp
from jax import lax
from jax.experimental import pallas as pl
from jax.experimental.pallas import tpu as pltpu
from jax.sharding import Mesh
from jax.sharding import PartitionSpec as P

KB = 4
KB2 = 8
BS = 128
ROWS = 16
COLS = 32
BF = jnp.bfloat16
F32 = jnp.float32

gelu_scale = 0.7978845608028654
cubic_term = 0.044715


def gelu_both(values):
    tangent = jnp.tanh(gelu_scale * (values + cubic_term * values * values * values))
    value = 0.5 * values * (1.0 + tangent)
    slope = 0.5 * (1.0 + tangent) + 0.5 * values * (1.0 - tangent * tangent) * gelu_scale * (
        1.0 + 3.0 * cubic_term * values * values
    )
    return value, slope


SMEM = pl.BlockSpec(memory_space=pltpu.SMEM)
VMEM = pl.BlockSpec(memory_space=pltpu.VMEM)


def call(kernel, scalars, arrays, outs, scratch=(), flops=1.1e9, name=None):
    moved = sum(a.size * a.dtype.itemsize for a in arrays)
    return pl.pallas_call(
        kernel,
        out_shape=outs,
        in_specs=[SMEM] * len(scalars) + [VMEM] * len(arrays),
        out_specs=[VMEM] * len(outs),
        scratch_shapes=list(scratch),
        compiler_params=pltpu.CompilerParams(vmem_limit_bytes=28 * 2**20),
        cost_estimate=pl.CostEstimate(flops=int(flops), bytes_accessed=int(moved), transcendentals=0),
        name=name,
    )(*scalars, *arrays)


def lanes(half):
    return pl.ds(pl.multiple_of(half * BS, BS), BS)


def block(ref, at):
    return ref[at // 2, :, lanes(at % 2)]


def up_kernel(order, where, x, w, *outs):
    for slot, out in enumerate(outs):

        def step(jj, carry):
            j = order[slot * 8 + jj]
            lhs = jnp.concatenate([block(x, where[j * KB + k]) for k in range(KB)], axis=1)
            rhs = w[pl.ds(j * KB, KB)].reshape(KB * BS, BS)
            out[jj] = jnp.dot(lhs, rhs, preferred_element_type=F32).astype(BF)
            return carry

        lax.fori_loop(0, 8, step, 0, unroll=4)


def add_back(acc, run, where, width, rows, w):
    rhs = w[pl.ds(run * width, width)].reshape(width * BS, BS)
    got = lax.dot_general(rows, rhs, (((1,), (1,)), ((), ())), preferred_element_type=F32)
    for k in range(width):
        at = where[run * width + k]
        acc[at] = acc[at] + got[:, k * BS:(k + 1) * BS]


def back_kernel(order, where, g, w, *rest):
    outs, acc = rest[:-1], rest[-1]
    acc[...] = jnp.zeros_like(acc)

    def step(at, carry):
        add_back(acc, order[at], where, KB2, block(g, at), w)
        return carry

    lax.fori_loop(0, ROWS, step, 0, unroll=2)
    for o, out in enumerate(outs):
        out[...] = acc[o * 4:(o + 1) * 4].astype(BF)


def act_kernel(place, p0, p1, p2, p3, active, slope, own, other, turned):
    z, q = place[0], place[1]

    def step(b, carry):
        hidden = p0[b].astype(F32) + p1[b].astype(F32) + p2[b].astype(F32) + p3[b].astype(F32)
        value, slopes = gelu_both(hidden)
        slope[b] = slopes
        value = value.astype(BF)
        active[b] = value
        rows = value.T.reshape(4, 2, 16, BS)
        for zz in range(4):
            at = jnp.bitwise_and(zz - z + 4, 3)
            for side in range(2):
                turned[jnp.bitwise_xor(side, q), at, b] = rows[zz, side]
        return carry

    lax.fori_loop(0, 8, step, 0, unroll=2)
    own[...] = turned[0]
    other[...] = turned[1]


def turn_kernel(place, x, x2, out):
    z, q = place[0], place[1]

    def step(p, carry):
        for half in range(2):
            for group, ref in enumerate((x, x2)):
                rows = ref[p, :, half * BS:(half + 1) * BS].T.reshape(4, 2, 16, BS)
                for zz in range(4):
                    mine = jnp.where(q == 0, rows[zz, 0], rows[zz, 1])
                    out[p * 2 + half, jnp.bitwise_xor(zz, z), :, group * BS:(group + 1) * BS] = mine
        return carry

    lax.fori_loop(0, 8, step, 0, unroll=2)


def up_terms_kernel(chunk, place, where, xt, v0, v1, near, far):
    r = place[2]

    def step(n, carry):
        row, jj = n // 4, n % 4
        j = row * 8 + chunk * 4 + jj
        at = jnp.bitwise_and(row - r + 4, 3) * 4 + jj
        lhs = jnp.concatenate([xt[where[j * KB + k]].reshape(64, 2 * BS) for k in range(KB)], axis=0)
        rhs = jnp.concatenate([v0[at], v1[at]], axis=0)
        got = jnp.dot(lhs, rhs, preferred_element_type=F32).astype(BF).reshape(KB, 4, 16, BS)
        for s, out in enumerate((near, far, near, far)):
            out[s // 2, pl.ds(n * KB, KB)] = got[:, s]
        return carry

    lax.fori_loop(0, 16, step, 0, unroll=2)


def down_terms_kernel(spot, where, a, g0, g1, f0, f1, out):
    def step(i, carry):
        at = spot[i]
        runs = [where[i * KB2 + k] for k in range(KB2)]
        lhs, rhs = [], []
        for tq, (g, f) in enumerate(((g0, f0), (g1, f1))):
            for tz in range(4):
                lhs.append(jnp.concatenate([a[u // 8, tz, tq, u % 8] for u in runs], axis=0))
                rhs.append(block(g, at) if tz == 0 else f[at // 4, tz - 1, at // 2 % 2, :, lanes(at % 2)])
        got = jnp.dot(jnp.concatenate(lhs, axis=1), jnp.concatenate(rhs, axis=0), preferred_element_type=F32)
        out[pl.ds(i * KB2, KB2)] = got.reshape(KB2, 16, BS)
        return carry

    lax.fori_loop(0, ROWS, step, 0, unroll=2)


def down_kernel(order, where, a, w, *outs):
    for slot, out in enumerate(outs):
        for t in range(2):
            for half in range(2):
                i = order[slot * 4 + t * 2 + half]
                lhs = jnp.concatenate([a[where[i * KB2 + k]] for k in range(KB2)], axis=1)
                rhs = w[pl.ds(i * KB2, KB2)].reshape(KB2 * BS, BS)
                out[t, :, half * BS:(half + 1) * BS] = jnp.dot(lhs, rhs, preferred_element_type=F32).astype(BF)


def into_kernel(order, where, v0, v1, w, *rest):
    outs, acc = rest[:-1], rest[-1]
    acc[...] = jnp.zeros_like(acc)
    for chunk, v in enumerate((v0, v1)):

        def step(at, carry):
            add_back(acc, order[at // 4 * 8 + chunk * 4 + at % 4], where, KB, v[at], w)
            return carry

        lax.fori_loop(0, 16, step, 0, unroll=4)
    for slot, out in enumerate(outs):
        for t in range(2):
            for half in range(2):
                out[t, :, half * BS:(half + 1) * BS] = acc[slot * 4 + t * 2 + half].astype(BF)


def shift(value, axis, size, by):
    return lax.ppermute(value, axis, [(i, (i + by) % size) for i in range(size)])


def swap(value, axis):
    return lax.ppermute(value, axis, [(0, 1), (1, 0)])


def across(value, by):
    return lax.ppermute(value, "z", [(i, i ^ by) for i in range(4)])


def after(value, *events):
    return lax.optimization_barrier((value, *events))[0]


def spread(own, axis):
    return jnp.concatenate([own] + [shift(own, axis, 4, -s) for s in (1, 2, 3)], axis=0)


def exchange(parts, axis):
    return [parts[0]] + [shift(parts[s], axis, 4, s) for s in (1, 2, 3)]


def total(parts):
    return sum((p.astype(F32) for p in parts[1:]), parts[0].astype(F32))


def scatter_features(parts):
    mine = total(exchange(parts, "y"))
    return (mine[0] + swap(mine[1].astype(BF), "h").astype(F32)).astype(BF)


def local(inputs, grad_out, up_blocks, up_index, down_blocks, down_index):
    z, q, r, h, y = (lax.axis_index(a).astype(jnp.int32) for a in ("z", "q", "row", "h", "y"))
    place = jnp.stack([z, q, r])
    c = h * 4 + y

    def feature_spot(b):
        return ((b // 2 % 4 - y) % 4) * 4 + jnp.bitwise_xor(b // 8, h) * 2 + b % 2

    def feature_at(s):
        return jnp.bitwise_xor(s // 2 % 2, h) * 8 + ((s // 4 + y) % 4) * 2 + s % 2

    def hidden_spot(f):
        return ((f // 8 - r) % 4) * 8 + f % 8

    def hidden_at(s):
        return ((s // 8 + r) % 4) * 8 + s % 8

    features, units = jnp.arange(ROWS, dtype=jnp.int32), jnp.arange(COLS, dtype=jnp.int32)
    up_where = feature_spot(up_index - r * ROWS)
    down_where = hidden_spot(down_index - c * COLS)
    feature_spots, feature_order = feature_spot(features), feature_at(features)
    hidden_order = hidden_at(units)

    def shape(*dims, dtype=BF):
        return jax.ShapeDtypeStruct(dims, dtype)

    x_own = jnp.stack([inputs, swap(inputs, "h")])
    g_own = jnp.stack([grad_out, swap(grad_out, "h")])
    x, g = spread(x_own, "y"), spread(g_own, "y")

    up = call(up_kernel, (hidden_order, up_where), (x, up_blocks), [shape(8, BS, BS)] * 4, name="up")
    back = call(
        back_kernel, (feature_order, down_where), (g, down_blocks), [shape(4, BS, BS)] * 8,
        [pltpu.VMEM((COLS, BS, BS), F32)], name="back",
    )
    parts = exchange(up, "row")
    active_own, slope, rows_own, rows_other = call(
        act_kernel, (place,), parts,
        [shape(8, BS, BS), shape(8, BS, BS, dtype=F32)] + [shape(4, 8, 16, BS)] * 2,
        [pltpu.VMEM((2, 4, 8, 16, BS), BF)], flops=1e7, name="act",
    )
    x2 = swap(after(x, up[3]), "q")
    (turned,) = call(turn_kernel, (place,), (x, x2), [shape(ROWS, 4, 16, 2 * BS)], flops=1e7, name="turn")
    far = jnp.stack([shift(after(g_own, x, g), "z", 4, s) for s in (1, 2, 3)])
    slope = after(slope, far, turned)

    owns = []
    for chunk in range(2):
        owns.append((total(exchange(back[chunk::2], "row")) * slope[chunk * 4:chunk * 4 + 4]).astype(BF))
        slope = after(slope, owns[0])
    grads, peers, terms = [], [], []
    for chunk in range(2):
        grads.append(spread(owns[chunk], "row"))
        peers.append(swap(grads[chunk], "q"))
        terms.append(call(
            lambda *a: up_terms_kernel(chunk, *a), (place, up_where), (turned, grads[chunk], peers[chunk]),
            [shape(2, 64, 16, BS)] * 2, flops=5e8, name="up_terms",
        ))
    rows_peer = swap(after(rows_other, owns[1]), "q")
    rows = exchange([jnp.stack([rows_own[s], rows_peer[s]]) for s in range(4)], "z")

    halves, firsts = [], []
    for near, other in terms:
        got = across(other, 1)
        firsts.append(got)
        keep = near[0].astype(F32) + got[0].astype(F32)
        send = (near[1].astype(F32) + got[1].astype(F32)).astype(BF)
        halves.append((keep, across(send, 2)))
    grad_up = jnp.concatenate(
        [(keep + got.astype(F32)).reshape(4, 1, 16, 16, BS) for keep, got in halves], axis=1
    ).reshape(128, 16, BS)

    far = spread(after(far[None], firsts[0]), "y")
    active = spread(after(active_own, terms[1][1]), "row")
    into = call(
        into_kernel, (hidden_order, up_where), (after(grads[0], firsts[0]), grads[1], up_blocks),
        [shape(2, BS, 2 * BS)] * 4, [pltpu.VMEM((ROWS, BS, BS), F32)], name="into",
    )
    grad_in = scatter_features(into)
    down = call(
        down_kernel, (feature_order, down_where), (after(active, firsts[0]), down_blocks),
        [shape(2, BS, 2 * BS)] * 4, name="down",
    )
    outputs = scatter_features(down)

    rows = spread(after(jnp.stack(rows)[None], active, firsts[0]), "row")
    g1, far1 = swap(after(g, firsts[1]), "q"), swap(after(far, firsts[1]), "q")
    (grad_down,) = call(
        down_terms_kernel, (feature_spots, down_where), (rows, g, g1, far, far1),
        [shape(128, 16, BS, dtype=F32)], name="down_terms",
    )
    return outputs, grad_in, grad_up, grad_down


def solution(mesh):
    fine = Mesh(mesh.devices.reshape(4, 2, 4, 2, 4), ("z", "q", "row", "h", "y"))
    tokens, width = ("z", "q"), ("row", "h", "y")
    placed = (
        P(tokens, width),
        P(tokens, width),
        P(width, None, None),
        P(width),
        P(width, None, None),
        P(width),
    )
    return jax.shard_map(
        local,
        mesh=fine,
        in_specs=placed,
        out_specs=(P(tokens, width), P(tokens, width), P(width, tokens, None), P(width, tokens, None)),
        check_vma=False,
    )
```

```python
import jax
import jax.numpy as jnp
from jax import lax
from jax.experimental import pallas as pl
from jax.experimental.pallas import tpu as pltpu
from jax.sharding import Mesh
from jax.sharding import PartitionSpec as P

KB = 4
KB2 = 8
BS = 128
ROWS = 16
COLS = 32
BF = jnp.bfloat16
F32 = jnp.float32

gelu_scale = 0.7978845608028654
cubic_term = 0.044715


def gelu_both(values):
    tangent = jnp.tanh(gelu_scale * (values + cubic_term * values * values * values))
    value = 0.5 * values * (1.0 + tangent)
    slope = 0.5 * (1.0 + tangent) + 0.5 * values * (1.0 - tangent * tangent) * gelu_scale * (
        1.0 + 3.0 * cubic_term * values * values
    )
    return value, slope


SMEM = pl.BlockSpec(memory_space=pltpu.SMEM)
VMEM = pl.BlockSpec(memory_space=pltpu.VMEM)
HBM = pl.BlockSpec(memory_space=pltpu.HBM)


def call(kernel, scalars, arrays, outs, scratch=(), weights=(), flops=1.1e9, name=None):
    moved = sum(a.size * a.dtype.itemsize for a in (*arrays, *weights))
    held = [pltpu.VMEM(w.shape, w.dtype) for w in weights] + [pltpu.SemaphoreType.DMA((4,)) for w in weights]
    return pl.pallas_call(
        kernel,
        out_shape=outs,
        in_specs=[SMEM] * len(scalars) + [VMEM] * len(arrays) + [HBM] * len(weights),
        out_specs=[VMEM] * len(outs),
        scratch_shapes=list(scratch) + held,
        compiler_params=pltpu.CompilerParams(vmem_limit_bytes=62 * 2**20),
        cost_estimate=pl.CostEstimate(flops=int(flops), bytes_accessed=int(moved), transcendentals=0),
        name=name,
    )(*scalars, *arrays, *weights)


def fetch(source, held, sems, firsts):
    copies = []
    for n, first in enumerate(firsts):
        part = pl.ds(first, 32)
        copies.append(pltpu.make_async_copy(source.at[part], held.at[part], sems.at[n]))
        copies[-1].start()
    return copies


def lanes(half):
    return pl.ds(pl.multiple_of(half * BS, BS), BS)


def block(ref, at):
    return ref[at // 2, :, lanes(at % 2)]


def up_kernel(order, where, x0, x1, x2, x3, source, o0, o1, o2, o3, x, w, sems):
    outs = (o0, o1, o2, o3)
    copies = fetch(source, w, sems, [order[slot * 8] * KB for slot in range(4)])
    for n, piece in enumerate((x0, x1, x2, x3)):
        x[n * 2:n * 2 + 2] = piece[...]
    for slot in (1, 2, 3, 0):
        out = outs[slot]
        copies[slot].wait()

        def step(jj, carry):
            j = order[slot * 8 + jj]
            lhs = jnp.concatenate([block(x, where[j * KB + k]) for k in range(KB)], axis=1)
            rhs = w[pl.ds(j * KB, KB)].reshape(KB * BS, BS)
            out[jj] = jnp.dot(lhs, rhs, preferred_element_type=F32).astype(BF)
            return carry

        lax.fori_loop(0, 8, step, 0, unroll=4)


def add_back(acc, run, where, width, rows, w):
    rhs = w[pl.ds(run * width, width)].reshape(width * BS, BS)
    got = lax.dot_general(rows, rhs, (((1,), (1,)), ((), ())), preferred_element_type=F32)
    for k in range(width):
        at = where[run * width + k]
        acc[at] = acc[at] + got[:, k * BS:(k + 1) * BS]


def back_kernel(spot, where, g0, g1, g2, g3, source, o0, o1, o2, o3, g, acc, w, sems):
    copies = fetch(source, w, sems, [0, 32, 64, 96])
    for n, piece in enumerate((g0, g1, g2, g3)):
        g[n * 2:n * 2 + 2] = piece[...]
    acc[...] = jnp.zeros_like(acc)
    for part in range(4):
        copies[part].wait()

        def step(ii, carry):
            i = part * 4 + ii
            add_back(acc, i, where, KB2, block(g, spot[i]), w)
            return carry

        lax.fori_loop(0, 4, step, 0, unroll=2)
    for slot, out in enumerate((o0, o1, o2, o3)):
        out[...] = acc[slot * 8:(slot + 1) * 8].astype(BF)


def act_kernel(p0, p1, p2, p3, active, slope, rows):
    def step(b, carry):
        hidden = p0[b].astype(F32) + p1[b].astype(F32) + p2[b].astype(F32) + p3[b].astype(F32)
        value, slopes = gelu_both(hidden)
        slope[b] = slopes
        value = value.astype(BF)
        active[b] = value
        turned = value.T.reshape(8, 16, BS)
        for d in range(8):
            rows[d, b] = turned[d]
        return carry

    lax.fori_loop(0, 8, step, 0, unroll=2)


def turn_kernel(place, x, x2, out):
    z, q = place[0], place[1]

    def step(p, carry):
        for half in range(2):
            for group, ref in enumerate((x, x2)):
                rows = ref[p, :, half * BS:(half + 1) * BS].T.reshape(4, 2, 16, BS)
                for zz in range(4):
                    mine = jnp.where(q == 0, rows[zz, 0], rows[zz, 1])
                    out[p * 2 + half, jnp.bitwise_xor(zz, z), :, group * BS:(group + 1) * BS] = mine
        return carry

    lax.fori_loop(0, 8, step, 0, unroll=2)


def up_terms_kernel(spot, where, xt, v0, v1, *outs):
    for chunk in range(2):
        near, far = outs[chunk * 2:chunk * 2 + 2]

        def step(n, carry):
            j = chunk * 16 + n
            at = spot[j]
            lhs = jnp.concatenate([xt[where[j * KB + k]].reshape(64, 2 * BS) for k in range(KB)], axis=0)
            rhs = jnp.concatenate([v0[at], v1[at]], axis=0)
            got = jnp.dot(lhs, rhs, preferred_element_type=F32).astype(BF).reshape(KB, 4, 16, BS)
            for s, out in enumerate((near, far, near, far)):
                out[s // 2, pl.ds(n * KB, KB)] = got[:, s]
            return carry

        lax.fori_loop(0, 16, step, 0, unroll=2)


def ends_kernel(feature_order, spot, up_where, down_where, v, a0, a1, a2, a3, source1, source2, *rest):
    outs, a, acc, w1, w2, sems1, sems2 = rest[:4], *rest[4:]
    copies1 = fetch(source1, w1, sems1, [0, 32, 64, 96])
    copies2 = fetch(source2, w2, sems2, [0, 32, 64, 96])
    for n, piece in enumerate((a0, a1, a2, a3)):
        a[n * 16:n * 16 + 16] = piece[...]
    acc[...] = jnp.zeros_like(acc)
    for part in range(4):
        copies1[part].wait()

        def step(jj, carry):
            j = part * 8 + jj
            add_back(acc, j, up_where, KB, v[spot[j]], w1)
            return carry

        lax.fori_loop(0, 8, step, 0, unroll=4)
    for part in range(4):
        copies2[part].wait()
    for slot, out in enumerate(outs):
        for t in range(2):
            for half in range(2):
                loc = slot * 4 + t * 2 + half
                at = slice(half * BS, (half + 1) * BS)
                out[t, 1, :, at] = acc[loc].astype(BF)
                i = feature_order[loc]
                runs = [down_where[i * KB2 + k] for k in range(KB2)]
                lhs = jnp.concatenate([a[u // 8 * 16 + u % 8] for u in runs], axis=1)
                rhs = w2[pl.ds(i * KB2, KB2)].reshape(KB2 * BS, BS)
                out[t, 0, :, at] = jnp.dot(lhs, rhs, preferred_element_type=F32).astype(BF)


def down_terms_kernel(place, spot, where, a, g0, g1, f0, f1, out):
    z, q = place[0], place[1]

    def step(i, carry):
        at = spot[i]
        runs = [where[i * KB2 + k] for k in range(KB2)]
        lhs, rhs = [], []
        for tq, (g, f) in enumerate(((g0, f0), (g1, f1))):
            for tz in range(4):
                source = jnp.bitwise_xor(z, tz) * 2 + jnp.bitwise_xor(q, tq) + 8
                lhs.append(jnp.concatenate(
                    [a[u // 8 * 16 + source, pl.ds(pl.multiple_of(u % 8 * 16, 16), 16), :] for u in runs], axis=0
                ))
                rhs.append(block(g, at) if tz == 0 else f[at // 4, tz - 1, at // 2 % 2, :, lanes(at % 2)])
        got = jnp.dot(jnp.concatenate(lhs, axis=1), jnp.concatenate(rhs, axis=0), preferred_element_type=F32)
        out[pl.ds(i * KB2, KB2)] = got.reshape(KB2, 16, BS)
        return carry

    lax.fori_loop(0, ROWS, step, 0, unroll=2)


def close_kernel(n0, r0, s0, n1, r1, s1, out):
    for chunk, (near, got, last) in enumerate(((n0, r0, s0), (n1, r1, s1))):
        out[chunk * 64:chunk * 64 + 64] = near[0].astype(F32) + got[0].astype(F32) + last[...].astype(F32)


def shift(value, axis, by):
    return lax.ppermute(value, axis, [(i, (i + by) % 4) for i in range(4)])


def swap(value, axis):
    return lax.ppermute(value, axis, [(0, 1), (1, 0)])


def across(value, by):
    return lax.ppermute(value, "z", [(i, i ^ by) for i in range(4)])


def after(value, *events):
    return lax.optimization_barrier((value, *events))[0]


def pieces(own, axis):
    return [own] + [shift(own, axis, -s) for s in (1, 2, 3)]


def exchange(parts, axis):
    return [parts[0]] + [shift(parts[s], axis, s) for s in (1, 2, 3)]


def total(parts):
    return sum((p.astype(F32) for p in parts[1:]), parts[0].astype(F32))


def local(inputs, grad_out, up_blocks, up_index, down_blocks, down_index):
    z, q, r, h, y = (lax.axis_index(a).astype(jnp.int32) for a in ("z", "q", "row", "h", "y"))
    place = jnp.stack([z, q])
    c = h * 4 + y

    def feature_spot(b):
        return ((b // 2 % 4 - y) % 4) * 4 + jnp.bitwise_xor(b // 8, h) * 2 + b % 2

    def feature_at(s):
        return jnp.bitwise_xor(s // 2 % 2, h) * 8 + ((s // 4 + y) % 4) * 2 + s % 2

    def hidden_spot(f):
        return ((f // 8 - r) % 4) * 8 + f % 8

    def hidden_at(s):
        return ((s // 8 + r) % 4) * 8 + s % 8

    features, units = jnp.arange(ROWS, dtype=jnp.int32), jnp.arange(COLS, dtype=jnp.int32)
    up_where = feature_spot(up_index - r * ROWS)
    down_where = hidden_spot(down_index - c * COLS)
    feature_spots, feature_order = feature_spot(features), feature_at(features)
    hidden_spots, hidden_order = hidden_spot(units), hidden_at(units)

    def shape(*dims, dtype=BF):
        return jax.ShapeDtypeStruct(dims, dtype)

    x_own = jnp.stack([inputs, swap(inputs, "h")])
    g_own = jnp.stack([grad_out, swap(grad_out, "h")])
    panel, piece = shape(8, BS, 2 * BS), shape(8, BS, BS)

    features_in, cotangents = pieces(x_own, "y"), pieces(g_own, "y")
    features_in[0] = after(features_in[0], cotangents[1])
    *up, x = call(
        up_kernel, (hidden_order, up_where), features_in, [piece] * 4 + [panel], weights=(up_blocks,), name="up"
    )
    up = exchange(up, "row")
    far1 = across(after(g_own, x), 1)
    far2 = across(after(jnp.stack([g_own, far1]), up[1]), 2)
    cotangents[0] = after(cotangents[0], up[1])
    *back, g = call(
        back_kernel, (feature_spots, down_where), cotangents, [piece] * 4 + [panel],
        [pltpu.VMEM((COLS, BS, BS), F32)], weights=(down_blocks,), name="back",
    )
    back = exchange(back, "row")
    x2 = swap(after(x, g), "q")
    (turned,) = call(turn_kernel, (place,), (x, x2), [shape(ROWS, 4, 16, 2 * BS)], flops=1e7, name="turn")
    active, slope, rows = call(
        act_kernel, (), up, [piece, shape(8, BS, BS, dtype=F32), shape(8, 8, 16, BS)], flops=1e7, name="act"
    )
    rows = lax.all_to_all(after(rows, back[0]), ("z", "q"), 0, 0, tiled=True)
    slope = after(slope, rows, turned, far2)

    own = (total(back) * slope).astype(BF)
    hidden = jnp.concatenate(pieces(own, "row"), axis=0)
    far = pieces(jnp.concatenate([far1[None], far2])[None], "y")
    hidden2 = swap(after(hidden, far[1]), "q")
    far = jnp.concatenate(far, axis=0)

    near0, send0, near1, send1 = call(
        up_terms_kernel, (hidden_spots, up_where), (turned, hidden, hidden2), [shape(2, 64, 16, BS)] * 4, name="up_terms"
    )
    got0, got1 = across(send0, 1), across(send1, 1)
    both = jnp.concatenate([active, rows.reshape(8, BS, BS)])
    both = pieces(after(both, send0, far), "row")
    last0 = across((near0[1].astype(F32) + got0[1].astype(F32)).astype(BF), 2)
    last1 = across((near1[1].astype(F32) + got1[1].astype(F32)).astype(BF), 2)

    *ends, a = call(
        ends_kernel, (feature_order, hidden_spots, up_where, down_where), (after(hidden, got0), *both),
        [shape(2, 2, BS, 2 * BS)] * 4 + [shape(64, BS, BS)], [pltpu.VMEM((ROWS, BS, BS), F32)],
        weights=(up_blocks, down_blocks), flops=2.2e9, name="ends",
    )
    mine = total(exchange(ends, "y"))
    ends = (mine[0] + swap(mine[1].astype(BF), "h").astype(F32)).astype(BF)

    g2, far3 = swap(after(g, send0), "q"), swap(after(far, send0), "q")
    (grad_down,) = call(
        down_terms_kernel, (place, feature_spots, down_where), (a, g, g2, far, far3),
        [shape(128, 16, BS, dtype=F32)], name="down_terms",
    )
    (grad_up,) = call(
        close_kernel, (), (near0, got0, last0, near1, got1, last1), [shape(128, 16, BS, dtype=F32)], flops=1e6, name="close"
    )
    return ends[0], ends[1], grad_up, grad_down


def solution(mesh):
    fine = Mesh(mesh.devices.reshape(4, 2, 4, 2, 4), ("z", "q", "row", "h", "y"))
    tokens, width = ("z", "q"), ("row", "h", "y")
    placed = (
        P(tokens, width),
        P(tokens, width),
        P(width, None, None),
        P(width),
        P(width, None, None),
        P(width),
    )
    return jax.shard_map(
        local,
        mesh=fine,
        in_specs=placed,
        out_specs=(P(tokens, width), P(tokens, width), P(width, tokens, None), P(width, tokens, None)),
        check_vma=False,
    )
```

```python
import jax
import jax.numpy as jnp
from jax import lax
from jax.experimental import pallas as pl
from jax.experimental.pallas import tpu as pltpu
from jax.sharding import Mesh
from jax.sharding import PartitionSpec as P

KB = 4
KB2 = 8
BS = 128
ROWS = 16
COLS = 32
BF = jnp.bfloat16
F32 = jnp.float32

gelu_scale = 0.7978845608028654
cubic_term = 0.044715


def gelu_both(values):
    tangent = jnp.tanh(gelu_scale * (values + cubic_term * values * values * values))
    value = 0.5 * values * (1.0 + tangent)
    slope = 0.5 * (1.0 + tangent) + 0.5 * values * (1.0 - tangent * tangent) * gelu_scale * (
        1.0 + 3.0 * cubic_term * values * values
    )
    return value, slope


SMEM = pl.BlockSpec(memory_space=pltpu.SMEM)
VMEM = pl.BlockSpec(memory_space=pltpu.VMEM)


def call(kernel, scalars, arrays, outs, scratch=(), name=None):
    return pl.pallas_call(
        kernel,
        out_shape=outs,
        in_specs=[SMEM] * len(scalars) + [VMEM] * len(arrays),
        out_specs=[VMEM] * len(outs),
        scratch_shapes=list(scratch),
        compiler_params=pltpu.CompilerParams(vmem_limit_bytes=28 * 2**20),
        cost_estimate=pl.CostEstimate(flops=1024, bytes_accessed=1024, transcendentals=0),
        name=name,
    )(*scalars, *arrays)


def lanes(half):
    return pl.ds(pl.multiple_of(half * BS, BS), BS)


def block(ref, at):
    return ref[at // 2, :, lanes(at % 2)]


def add_back(acc, run, where, width, rows, w):
    rhs = w[pl.ds(run * width, width)].reshape(width * BS, BS)
    got = lax.dot_general(rows, rhs, (((1,), (1,)), ((), ())), preferred_element_type=F32)
    for k in range(width):
        at = where[run * width + k]
        acc[at] = acc[at] + got[:, k * BS:(k + 1) * BS]


def first_kernel(order, spot, up_where, down_where, x0, x1, x2, x3, g0, g1, g2, g3, w1, w2, *rest):
    outs, x, g, acc = rest[:4], *rest[4:]
    for n, piece in enumerate((x0, x1, x2, x3)):
        x[n * 2:n * 2 + 2] = piece[...]
    for n, piece in enumerate((g0, g1, g2, g3)):
        g[n * 2:n * 2 + 2] = piece[...]
    acc[...] = jnp.zeros_like(acc)

    def back(i, carry):
        add_back(acc, i, down_where, KB2, block(g, spot[i]), w2)
        return carry

    lax.fori_loop(0, ROWS, back, 0, unroll=2)
    for slot, out in enumerate(outs):
        out[1] = acc[slot * 8:(slot + 1) * 8].astype(BF)

        def up(jj, carry):
            j = order[slot * 8 + jj]
            lhs = jnp.concatenate([block(x, up_where[j * KB + k]) for k in range(KB)], axis=1)
            rhs = w1[pl.ds(j * KB, KB)].reshape(KB * BS, BS)
            out[0, jj] = jnp.dot(lhs, rhs, preferred_element_type=F32).astype(BF)
            return carry

        lax.fori_loop(0, 8, up, 0, unroll=4)


def act_kernel(p0, p1, p2, p3, active, own, rows):
    def step(b, carry):
        hidden, grad = (
            p0[n, b].astype(F32) + p1[n, b].astype(F32) + p2[n, b].astype(F32) + p3[n, b].astype(F32) for n in range(2)
        )
        value, slope = gelu_both(hidden)
        own[b] = (grad * slope).astype(BF)
        value = value.astype(BF)
        active[b] = value
        turned = value.T.reshape(8, 16, BS)
        for d in range(8):
            rows[d, b] = turned[d]
        return carry

    lax.fori_loop(0, 8, step, 0, unroll=2)


def turn_kernel(place, x, x2, out):
    z, q = place[0], place[1]

    def step(p, carry):
        for half in range(2):
            for group, ref in enumerate((x, x2)):
                rows = ref[p, :, half * BS:(half + 1) * BS].T.reshape(4, 2, 16, BS)
                for zz in range(4):
                    mine = jnp.where(q == 0, rows[zz, 0], rows[zz, 1])
                    out[p * 2 + half, jnp.bitwise_xor(zz, z), :, group * BS:(group + 1) * BS] = mine
        return carry

    lax.fori_loop(0, 8, step, 0, unroll=2)


def up_terms_kernel(spot, where, xt, v0, v1, *outs):
    for chunk in range(2):
        near, far = outs[chunk * 2:chunk * 2 + 2]

        def step(n, carry):
            j = chunk * 16 + n
            at = spot[j]
            lhs = jnp.concatenate([xt[where[j * KB + k]].reshape(64, 2 * BS) for k in range(KB)], axis=0)
            rhs = jnp.concatenate([v0[at], v1[at]], axis=0)
            got = jnp.dot(lhs, rhs, preferred_element_type=F32).astype(BF).reshape(KB, 4, 16, BS)
            for s, out in enumerate((near, far, near, far)):
                out[s // 2, pl.ds(n * KB, KB)] = got[:, s]
            return carry

        lax.fori_loop(0, 16, step, 0, unroll=2)


def into_kernel(spot, where, v, w, o0, o1, o2, o3, acc):
    acc[...] = jnp.zeros_like(acc)

    def step(j, carry):
        add_back(acc, j, where, KB, v[spot[j]], w)
        return carry

    lax.fori_loop(0, COLS, step, 0, unroll=4)
    for slot, out in enumerate((o0, o1, o2, o3)):
        for t in range(2):
            for half in range(2):
                out[t, :, half * BS:(half + 1) * BS] = acc[slot * 4 + t * 2 + half].astype(BF)


def down_kernel(order, where, a0, a1, a2, a3, w, o0, o1, o2, o3, a):
    for n, piece in enumerate((a0, a1, a2, a3)):
        a[n * 16:n * 16 + 16] = piece[...]
    for slot, out in enumerate((o0, o1, o2, o3)):
        for t in range(2):
            for half in range(2):
                i = order[slot * 4 + t * 2 + half]
                runs = [where[i * KB2 + k] for k in range(KB2)]
                lhs = jnp.concatenate([a[u // 8 * 16 + u % 8] for u in runs], axis=1)
                rhs = w[pl.ds(i * KB2, KB2)].reshape(KB2 * BS, BS)
                out[t, :, half * BS:(half + 1) * BS] = jnp.dot(lhs, rhs, preferred_element_type=F32).astype(BF)


def down_terms_kernel(place, spot, where, a, g0, g1, f0, f1, out):
    z, q = place[0], place[1]

    def step(i, carry):
        at = spot[i]
        runs = [where[i * KB2 + k] for k in range(KB2)]
        lhs, rhs = [], []
        for tq, (g, f) in enumerate(((g0, f0), (g1, f1))):
            for tz in range(4):
                source = jnp.bitwise_xor(z, tz) * 2 + jnp.bitwise_xor(q, tq) + 8
                lhs.append(jnp.concatenate(
                    [a[u // 8 * 16 + source, pl.ds(pl.multiple_of(u % 8 * 16, 16), 16), :] for u in runs], axis=0
                ))
                rhs.append(block(g, at) if tz == 0 else f[at // 4, tz - 1, at // 2 % 2, :, lanes(at % 2)])
        got = jnp.dot(jnp.concatenate(lhs, axis=1), jnp.concatenate(rhs, axis=0), preferred_element_type=F32)
        out[pl.ds(i * KB2, KB2)] = got.reshape(KB2, 16, BS)
        return carry

    lax.fori_loop(0, ROWS, step, 0, unroll=2)


def close_kernel(n0, r0, s0, n1, r1, s1, out):
    for chunk, (near, got, last) in enumerate(((n0, r0, s0), (n1, r1, s1))):
        out[chunk * 64:chunk * 64 + 64] = near[0].astype(F32) + got[0].astype(F32) + last[...].astype(F32)


def shift(value, axis, by):
    return lax.ppermute(value, axis, [(i, (i + by) % 4) for i in range(4)])


def swap(value, axis):
    return lax.ppermute(value, axis, [(0, 1), (1, 0)])


def across(value, by):
    return lax.ppermute(value, "z", [(i, i ^ by) for i in range(4)])


def after(value, *events):
    return lax.optimization_barrier((value, *events))[0]


def pieces(own, axis):
    return [own] + [shift(own, axis, -s) for s in (1, 2, 3)]


def exchange(parts, axis):
    return [parts[0]] + [shift(parts[s], axis, s) for s in (1, 2, 3)]


def scatter_features(parts):
    mine = total(exchange(parts, "y"))
    return (mine[0] + swap(mine[1].astype(BF), "h").astype(F32)).astype(BF)


def total(parts):
    return sum((p.astype(F32) for p in parts[1:]), parts[0].astype(F32))


def local(inputs, grad_out, up_blocks, up_index, down_blocks, down_index):
    z, q, r, h, y = (lax.axis_index(a).astype(jnp.int32) for a in ("z", "q", "row", "h", "y"))
    place = jnp.stack([z, q])
    c = h * 4 + y

    def feature_spot(b):
        return ((b // 2 % 4 - y) % 4) * 4 + jnp.bitwise_xor(b // 8, h) * 2 + b % 2

    def feature_at(s):
        return jnp.bitwise_xor(s // 2 % 2, h) * 8 + ((s // 4 + y) % 4) * 2 + s % 2

    def hidden_spot(f):
        return ((f // 8 - r) % 4) * 8 + f % 8

    def hidden_at(s):
        return ((s // 8 + r) % 4) * 8 + s % 8

    features, units = jnp.arange(ROWS, dtype=jnp.int32), jnp.arange(COLS, dtype=jnp.int32)
    up_where = feature_spot(up_index - r * ROWS)
    down_where = hidden_spot(down_index - c * COLS)
    feature_spots, feature_order = feature_spot(features), feature_at(features)
    hidden_spots, hidden_order = hidden_spot(units), hidden_at(units)

    def shape(*dims, dtype=BF):
        return jax.ShapeDtypeStruct(dims, dtype)

    x_own = jnp.stack([inputs, swap(inputs, "h")])
    g_own = jnp.stack([grad_out, swap(grad_out, "h")])
    panel, piece = shape(8, BS, 2 * BS), shape(8, BS, BS)

    *parts, x, g = call(
        first_kernel, (hidden_order, feature_spots, up_where, down_where),
        (*pieces(x_own, "y"), *pieces(g_own, "y"), up_blocks, down_blocks),
        [shape(2, 8, BS, BS)] * 4 + [panel] * 2, [pltpu.VMEM((COLS, BS, BS), F32)], name="first",
    )
    parts = exchange(parts, "row")
    far1 = across(after(g_own, x), 1)
    far2 = across(jnp.stack([g_own, far1]), 2)
    x2, g2 = swap(x, "q"), swap(g, "q")
    (turned,) = call(turn_kernel, (place,), (x, x2), [shape(ROWS, 4, 16, 2 * BS)], name="turn")
    parts[0] = after(parts[0], turned, far2, g2)
    active, own, rows = call(act_kernel, (), parts, [piece, piece, shape(8, 8, 16, BS)], name="act")

    rows = lax.all_to_all(rows, ("z", "q"), 0, 0, tiled=True)
    hidden = jnp.concatenate(pieces(own, "row"), axis=0)
    far = pieces(after(jnp.concatenate([far1[None], far2])[None], own), "y")
    hidden2 = swap(after(hidden, rows, *far[1:]), "q")

    slab = shape(2, BS, 2 * BS)
    into = call(
        into_kernel, (hidden_spots, up_where), (hidden, up_blocks), [slab] * 4, [pltpu.VMEM((ROWS, BS, BS), F32)], name="into"
    )
    turned = after(turned, into[0])
    near0, send0, near1, send1 = call(
        up_terms_kernel, (hidden_spots, up_where), (turned, hidden, hidden2), [shape(2, 64, 16, BS)] * 4, name="up_terms"
    )
    got0, got1 = across(send0, 1), across(send1, 1)
    both = jnp.concatenate([active, rows.reshape(8, BS, BS)])
    both = pieces(after(both, send0), "row")
    last0 = across((near0[1].astype(F32) + got0[1].astype(F32)).astype(BF), 2)
    send2 = (near1[1].astype(F32) + got1[1].astype(F32)).astype(BF)
    last1 = across(send2, 2)
    both[0] = after(both[0], last0, send2)
    *down, a = call(
        down_kernel, (feature_order, down_where), (*both, down_blocks), [slab] * 4 + [shape(64, BS, BS)], name="down"
    )
    outputs = scatter_features(down)
    grad_in = scatter_features(lax.optimization_barrier((*into, got0))[:4])

    far = jnp.concatenate(far, axis=0)
    far3 = swap(after(far, got0), "q")
    (grad_down,) = call(
        down_terms_kernel, (place, feature_spots, down_where), (a, g, g2, far, far3),
        [shape(128, 16, BS, dtype=F32)], name="down_terms",
    )
    (grad_up,) = call(
        close_kernel, (), (after(near0, grad_down), got0, last0, near1, got1, last1), [shape(128, 16, BS, dtype=F32)], name="close"
    )
    return outputs, grad_in, grad_up, grad_down


def solution(mesh):
    fine = Mesh(mesh.devices.reshape(4, 2, 4, 2, 4), ("z", "q", "row", "h", "y"))
    tokens, width = ("z", "q"), ("row", "h", "y")
    placed = (
        P(tokens, width),
        P(tokens, width),
        P(width, None, None),
        P(width),
        P(width, None, None),
        P(width),
    )
    return jax.shard_map(
        local,
        mesh=fine,
        in_specs=placed,
        out_specs=(P(tokens, width), P(tokens, width), P(width, tokens, None), P(width, tokens, None)),
        check_vma=False,
    )
```

```python
import jax
import jax.numpy as jnp
from jax import lax
from jax.experimental import pallas as pl
from jax.experimental.pallas import tpu as pltpu
from jax.sharding import Mesh
from jax.sharding import PartitionSpec as P

KB = 4
KB2 = 8
BS = 128
ROWS = 16
COLS = 32
BF = jnp.bfloat16
F32 = jnp.float32

gelu_scale = 0.7978845608028654
cubic_term = 0.044715


def gelu_both(values):
    tangent = jnp.tanh(gelu_scale * (values + cubic_term * values * values * values))
    value = 0.5 * values * (1.0 + tangent)
    slope = 0.5 * (1.0 + tangent) + 0.5 * values * (1.0 - tangent * tangent) * gelu_scale * (
        1.0 + 3.0 * cubic_term * values * values
    )
    return value, slope


SMEM = pl.BlockSpec(memory_space=pltpu.SMEM)
VMEM = pl.BlockSpec(memory_space=pltpu.VMEM)


def call(kernel, scalars, arrays, outs, scratch=(), name=None):
    return pl.pallas_call(
        kernel,
        out_shape=outs,
        in_specs=[SMEM] * len(scalars) + [VMEM] * len(arrays),
        out_specs=[VMEM] * len(outs),
        scratch_shapes=list(scratch),
        compiler_params=pltpu.CompilerParams(vmem_limit_bytes=20 * 2**20),
        cost_estimate=pl.CostEstimate(flops=1024, bytes_accessed=1024, transcendentals=0),
        name=name,
    )(*scalars, *arrays)


def lanes(half):
    return pl.ds(pl.multiple_of(half * BS, BS), BS)


def block(ref, at):
    return ref[at // 2, :, lanes(at % 2)]


def add_back(acc, run, where, width, rows, w):
    rhs = w[pl.ds(run * width, width)].reshape(width * BS, BS)
    got = lax.dot_general(rows, rhs, (((1,), (1,)), ((), ())), preferred_element_type=F32)
    for k in range(width):
        at = where[run * width + k]
        acc[at] = acc[at] + got[:, k * BS:(k + 1) * BS]


def first_kernel(order, spot, up_where, down_where, x0, x1, x2, x3, g0, g1, g2, g3, w1, w2, *rest):
    outs, x, g, acc = rest[:4], *rest[4:]
    for n, piece in enumerate((x0, x1, x2, x3)):
        x[n * 2:n * 2 + 2] = piece[...]
    for n, piece in enumerate((g0, g1, g2, g3)):
        g[n * 2:n * 2 + 2] = piece[...]
    acc[...] = jnp.zeros_like(acc)

    def back(i, carry):
        add_back(acc, i, down_where, KB2, block(g, spot[i]), w2)
        return carry

    lax.fori_loop(0, ROWS, back, 0, unroll=2)
    for slot, out in enumerate(outs):
        out[1] = acc[slot * 8:(slot + 1) * 8].astype(BF)

        def up(jj, carry):
            j = order[slot * 8 + jj]
            lhs = jnp.concatenate([block(x, up_where[j * KB + k]) for k in range(KB)], axis=1)
            rhs = w1[pl.ds(j * KB, KB)].reshape(KB * BS, BS)
            out[0, jj] = jnp.dot(lhs, rhs, preferred_element_type=F32).astype(BF)
            return carry

        lax.fori_loop(0, 8, up, 0, unroll=4)


def act_kernel(p0, p1, p2, p3, active, own, rows):
    def step(b, carry):
        hidden, grad = (
            p0[n, b].astype(F32) + p1[n, b].astype(F32) + p2[n, b].astype(F32) + p3[n, b].astype(F32) for n in range(2)
        )
        value, slope = gelu_both(hidden)
        own[b] = (grad * slope).astype(BF)
        value = value.astype(BF)
        active[b] = value
        turned = value.T.reshape(8, 16, BS)
        for d in range(8):
            rows[d, b] = turned[d]
        return carry

    lax.fori_loop(0, 8, step, 0, unroll=2)


def turn_kernel(place, x, x2, out):
    z, q = place[0], place[1]

    def step(p, carry):
        for half in range(2):
            for group, ref in enumerate((x, x2)):
                rows = ref[p, :, half * BS:(half + 1) * BS].T.reshape(4, 2, 16, BS)
                for zz in range(4):
                    mine = jnp.where(q == 0, rows[zz, 0], rows[zz, 1])
                    out[p * 2 + half, jnp.bitwise_xor(zz, z), :, group * BS:(group + 1) * BS] = mine
        return carry

    lax.fori_loop(0, 8, step, 0, unroll=2)


def join_kernel(p0, p1, p2, p3, out):
    size = p0.shape[0]
    for n, piece in enumerate((p0, p1, p2, p3)):
        out[n * size:(n + 1) * size] = piece[...]


def join(parts):
    first = parts[0]
    whole = jax.ShapeDtypeStruct((4 * first.shape[0], *first.shape[1:]), first.dtype)
    return call(join_kernel, (), parts, [whole], name="join")[0]


def up_terms_kernel(spot, where, xt, v0, v1, near, far):
    def step(j, carry):
        at = spot[j]
        lhs = jnp.concatenate([xt[where[j * KB + k]].reshape(64, 2 * BS) for k in range(KB)], axis=0)
        rhs = jnp.concatenate([v0[at], v1[at]], axis=0)
        got = jnp.dot(lhs, rhs, preferred_element_type=F32).astype(BF).reshape(KB, 4, 16, BS)
        for s, out in enumerate((near, far, near, far)):
            out[s // 2, pl.ds(j * KB, KB)] = got[:, s]
        return carry

    lax.fori_loop(0, COLS, step, 0, unroll=2)


def into_kernel(spot, where, v, w, o0, o1, o2, o3, acc):
    acc[...] = jnp.zeros_like(acc)

    def step(j, carry):
        add_back(acc, j, where, KB, v[spot[j]], w)
        return carry

    lax.fori_loop(0, COLS, step, 0, unroll=4)
    for slot, out in enumerate((o0, o1, o2, o3)):
        for t in range(2):
            for half in range(2):
                out[t, :, half * BS:(half + 1) * BS] = acc[slot * 4 + t * 2 + half].astype(BF)


def down_kernel(order, where, a0, a1, a2, a3, w, o0, o1, o2, o3, a):
    for n, piece in enumerate((a0, a1, a2, a3)):
        a[n * 16:n * 16 + 16] = piece[...]
    for slot, out in enumerate((o0, o1, o2, o3)):
        for t in range(2):
            for half in range(2):
                i = order[slot * 4 + t * 2 + half]
                runs = [where[i * KB2 + k] for k in range(KB2)]
                lhs = jnp.concatenate([a[u // 8 * 16 + u % 8] for u in runs], axis=1)
                rhs = w[pl.ds(i * KB2, KB2)].reshape(KB2 * BS, BS)
                out[t, :, half * BS:(half + 1) * BS] = jnp.dot(lhs, rhs, preferred_element_type=F32).astype(BF)


def down_terms_kernel(place, spot, where, a, g0, g1, f0, f1, out):
    z, q = place[0], place[1]

    def step(i, carry):
        at = spot[i]
        runs = [where[i * KB2 + k] for k in range(KB2)]
        lhs, rhs = [], []
        for tq, (g, f) in enumerate(((g0, f0), (g1, f1))):
            for tz in range(4):
                source = jnp.bitwise_xor(z, tz) * 2 + jnp.bitwise_xor(q, tq) + 8
                lhs.append(jnp.concatenate(
                    [a[u // 8 * 16 + source, pl.ds(pl.multiple_of(u % 8 * 16, 16), 16), :] for u in runs], axis=0
                ))
                rhs.append(block(g, at) if tz == 0 else f[at // 4, tz - 1, at // 2 % 2, :, lanes(at % 2)])
        got = jnp.dot(jnp.concatenate(lhs, axis=1), jnp.concatenate(rhs, axis=0), preferred_element_type=F32)
        out[pl.ds(i * KB2, KB2)] = got.reshape(KB2, 16, BS)
        return carry

    lax.fori_loop(0, ROWS, step, 0, unroll=2)


def close_kernel(near, got, last, out):
    out[...] = near[0].astype(F32) + got[0].astype(F32) + last[...].astype(F32)


def shift(value, axis, by):
    return lax.ppermute(value, axis, [(i, (i + by) % 4) for i in range(4)])


def swap(value, axis):
    return lax.ppermute(value, axis, [(0, 1), (1, 0)])


def across(value, by):
    return lax.ppermute(value, "z", [(i, i ^ by) for i in range(4)])


def after(value, *events):
    return lax.optimization_barrier((value, *events))[0]


def pieces(own, axis):
    return [own] + [shift(own, axis, -s) for s in (1, 2, 3)]


def exchange(parts, axis):
    return [parts[0]] + [shift(parts[s], axis, s) for s in (1, 2, 3)]


def scatter_features(parts):
    mine = total(exchange(parts, "y"))
    return (mine[0] + swap(mine[1].astype(BF), "h").astype(F32)).astype(BF)


def total(parts):
    return sum((p.astype(F32) for p in parts[1:]), parts[0].astype(F32))


def local(inputs, grad_out, up_blocks, up_index, down_blocks, down_index):
    z, q, r, h, y = (lax.axis_index(a).astype(jnp.int32) for a in ("z", "q", "row", "h", "y"))
    place = jnp.stack([z, q])
    c = h * 4 + y

    def feature_spot(b):
        return ((b // 2 % 4 - y) % 4) * 4 + jnp.bitwise_xor(b // 8, h) * 2 + b % 2

    def feature_at(s):
        return jnp.bitwise_xor(s // 2 % 2, h) * 8 + ((s // 4 + y) % 4) * 2 + s % 2

    def hidden_spot(f):
        return ((f // 8 - r) % 4) * 8 + f % 8

    def hidden_at(s):
        return ((s // 8 + r) % 4) * 8 + s % 8

    features, units = jnp.arange(ROWS, dtype=jnp.int32), jnp.arange(COLS, dtype=jnp.int32)
    up_where = feature_spot(up_index - r * ROWS)
    down_where = hidden_spot(down_index - c * COLS)
    feature_spots, feature_order = feature_spot(features), feature_at(features)
    hidden_spots, hidden_order = hidden_spot(units), hidden_at(units)

    def shape(*dims, dtype=BF):
        return jax.ShapeDtypeStruct(dims, dtype)

    x_own = jnp.stack([inputs, swap(inputs, "h")])
    g_own = jnp.stack([grad_out, swap(grad_out, "h")])
    panel, piece = shape(8, BS, 2 * BS), shape(8, BS, BS)

    far1 = across(after(g_own, x_own), 1)
    cotangents = pieces(g_own, "y")
    cotangents[0] = after(cotangents[0], far1)
    *parts, x, g = call(
        first_kernel, (hidden_order, feature_spots, up_where, down_where),
        (*pieces(x_own, "y"), *cotangents, up_blocks, down_blocks),
        [shape(2, 8, BS, BS)] * 4 + [panel] * 2, [pltpu.VMEM((COLS, BS, BS), F32)], name="first",
    )
    parts = exchange(parts, "row")
    far2 = across(after(jnp.stack([g_own, far1]), x), 2)
    x2 = swap(x, "q")
    (turned,) = call(turn_kernel, (place,), (x, x2), [shape(ROWS, 4, 16, 2 * BS)], name="turn")
    parts[0] = after(parts[0], far2, turned)
    active, own, rows = call(act_kernel, (), parts, [piece, piece, shape(8, 8, 16, BS)], name="act")
    far = pieces(after(jnp.concatenate([far1[None], far2])[None], own), "y")
    rows = lax.all_to_all(rows, ("z", "q"), 0, 0, tiled=True)
    hidden = join(pieces(own, "row"))
    hidden2 = swap(after(hidden, rows, *far[1:]), "q")
    near, send = call(
        up_terms_kernel, (hidden_spots, up_where), (turned, hidden, hidden2), [shape(2, 128, 16, BS)] * 2, name="up_terms"
    )
    got = across(send, 1)
    both = jnp.concatenate([active, rows.reshape(8, BS, BS)])
    both = pieces(after(both, send), "row")
    again = (near[1].astype(F32) + got[1].astype(F32)).astype(BF)
    last = across(again, 2)
    slab = shape(2, BS, 2 * BS)
    both[0] = after(both[0], again)
    *down, a = call(
        down_kernel, (feature_order, down_where), (*both, down_blocks), [slab] * 4 + [shape(64, BS, BS)], name="down"
    )
    into = call(
        into_kernel, (hidden_spots, up_where), (after(hidden, a), up_blocks), [slab] * 4,
        [pltpu.VMEM((ROWS, BS, BS), F32)], name="into",
    )
    grad_in = scatter_features(into)

    far[0] = after(far[0], send)
    far = join(far)
    g2 = swap(after(g, send), "q")
    (grad_down,) = call(
        down_terms_kernel, (place, feature_spots, down_where), (a, g, g2, far, swap(far, "q")),
        [shape(128, 16, BS, dtype=F32)], name="down_terms",
    )
    mine = total(exchange(down, "y"))
    outputs = (mine[0] + swap(after(mine[1].astype(BF), grad_down), "h").astype(F32)).astype(BF)
    (grad_up,) = call(close_kernel, (), (near, got, last), [shape(128, 16, BS, dtype=F32)], name="close")
    return outputs, grad_in, grad_up, grad_down


def solution(mesh):
    fine = Mesh(mesh.devices.reshape(4, 2, 4, 2, 4), ("z", "q", "row", "h", "y"))
    tokens, width = ("z", "q"), ("row", "h", "y")
    placed = (
        P(tokens, width),
        P(tokens, width),
        P(width, None, None),
        P(width),
        P(width, None, None),
        P(width),
    )
    return jax.shard_map(
        local,
        mesh=fine,
        in_specs=placed,
        out_specs=(P(tokens, width), P(tokens, width), P(width, tokens, None), P(width, tokens, None)),
        check_vma=False,
    )
```

```python
import jax
import jax.numpy as jnp
from jax import lax
from jax.experimental import pallas as pl
from jax.experimental.pallas import tpu as pltpu
from jax.sharding import Mesh
from jax.sharding import PartitionSpec as P

KB = 4
KB2 = 8
BS = 128
ROWS = 16
COLS = 32
BF = jnp.bfloat16
F32 = jnp.float32

gelu_scale = 0.7978845608028654
cubic_term = 0.044715


def gelu_both(values):
    tangent = jnp.tanh(gelu_scale * (values + cubic_term * values * values * values))
    value = 0.5 * values * (1.0 + tangent)
    slope = 0.5 * (1.0 + tangent) + 0.5 * values * (1.0 - tangent * tangent) * gelu_scale * (
        1.0 + 3.0 * cubic_term * values * values
    )
    return value, slope


SMEM = pl.BlockSpec(memory_space=pltpu.SMEM)
VMEM = pl.BlockSpec(memory_space=pltpu.VMEM)


def call(kernel, scalars, arrays, outs, scratch=(), name=None):
    return pl.pallas_call(
        kernel,
        out_shape=outs,
        in_specs=[SMEM] * len(scalars) + [VMEM] * len(arrays),
        out_specs=[VMEM] * len(outs),
        scratch_shapes=list(scratch),
        compiler_params=pltpu.CompilerParams(vmem_limit_bytes=28 * 2**20),
        cost_estimate=pl.CostEstimate(flops=1024, bytes_accessed=1024, transcendentals=0),
        name=name,
    )(*scalars, *arrays)


def lanes(half):
    return pl.ds(pl.multiple_of(half * BS, BS), BS)


def block(ref, at):
    return ref[at // 2, :, lanes(at % 2)]


def add_back(acc, run, where, width, rows, w):
    rhs = w[pl.ds(run * width, width)].reshape(width * BS, BS)
    got = lax.dot_general(rows, rhs, (((1,), (1,)), ((), ())), preferred_element_type=F32)
    for k in range(width):
        at = where[run * width + k]
        acc[at] = acc[at] + got[:, k * BS:(k + 1) * BS]


def first_kernel(order, spot, up_where, down_where, x0, x1, x2, x3, g0, g1, g2, g3, w1, w2, *rest):
    outs, x, g, acc = rest[:4], *rest[4:]
    for n, piece in enumerate((x0, x1, x2, x3)):
        x[n * 2:n * 2 + 2] = piece[...]
    for n, piece in enumerate((g0, g1, g2, g3)):
        g[n * 2:n * 2 + 2] = piece[...]
    acc[...] = jnp.zeros_like(acc)

    def back(i, carry):
        add_back(acc, i, down_where, KB2, block(g, spot[i]), w2)
        return carry

    lax.fori_loop(0, ROWS, back, 0, unroll=2)
    for slot, out in enumerate(outs):
        out[1] = acc[slot * 8:(slot + 1) * 8].astype(BF)

        def up(jj, carry):
            j = order[slot * 8 + jj]
            lhs = jnp.concatenate([block(x, up_where[j * KB + k]) for k in range(KB)], axis=1)
            rhs = w1[pl.ds(j * KB, KB)].reshape(KB * BS, BS)
            out[0, jj] = jnp.dot(lhs, rhs, preferred_element_type=F32).astype(BF)
            return carry

        lax.fori_loop(0, 8, up, 0, unroll=4)


def act_kernel(p0, p1, p2, p3, active, own, rows):
    def step(b, carry):
        hidden, grad = (
            p0[n, b].astype(F32) + p1[n, b].astype(F32) + p2[n, b].astype(F32) + p3[n, b].astype(F32) for n in range(2)
        )
        value, slope = gelu_both(hidden)
        own[b] = (grad * slope).astype(BF)
        value = value.astype(BF)
        active[b] = value
        turned = value.T.reshape(8, 16, BS)
        for d in range(8):
            rows[d, b] = turned[d]
        return carry

    lax.fori_loop(0, 8, step, 0, unroll=2)


def turn_kernel(place, x, x2, out):
    q = place[1]

    def step(p, carry):
        for half in range(2):
            for group, ref in enumerate((x, x2)):
                rows = ref[p, :, half * BS:(half + 1) * BS].T.reshape(4, 2, 16, BS)
                for zz in range(4):
                    mine = jnp.where(q == 0, rows[zz, 0], rows[zz, 1])
                    out[p * 2 + half, zz, :, group * BS:(group + 1) * BS] = mine
        return carry

    lax.fori_loop(0, 8, step, 0, unroll=2)


def join_kernel(p0, p1, p2, p3, out):
    size = p0.shape[0]
    for n, piece in enumerate((p0, p1, p2, p3)):
        out[n * size:(n + 1) * size] = piece[...]


def join(parts):
    first = parts[0]
    whole = jax.ShapeDtypeStruct((4 * first.shape[0], *first.shape[1:]), first.dtype)
    return call(join_kernel, (), parts, [whole], name="join")[0]


def up_terms_kernel(spot, where, xt, v0, v1, out):
    def step(j, carry):
        at = spot[j]
        lhs = jnp.concatenate([xt[where[j * KB + k]].reshape(64, 2 * BS) for k in range(KB)], axis=0)
        rhs = jnp.concatenate([v0[at], v1[at]], axis=0)
        got = jnp.dot(lhs, rhs, preferred_element_type=F32).astype(BF).reshape(KB, 4, 16, BS)
        for zz in range(4):
            out[zz, pl.ds(j * KB, KB)] = got[:, zz]
        return carry

    lax.fori_loop(0, COLS, step, 0, unroll=2)


def ends_kernel(order, spot, up_where, down_where, v, a0, a1, a2, a3, w1, w2, o0, o1, o2, o3, a, acc):
    for n, piece in enumerate((a0, a1, a2, a3)):
        a[n * 16:n * 16 + 16] = piece[...]
    acc[...] = jnp.zeros_like(acc)

    def step(j, carry):
        add_back(acc, j, up_where, KB, v[spot[j]], w1)
        return carry

    lax.fori_loop(0, COLS, step, 0, unroll=4)
    for slot, out in enumerate((o0, o1, o2, o3)):
        for t in range(2):
            for half in range(2):
                loc = slot * 4 + t * 2 + half
                at = slice(half * BS, (half + 1) * BS)
                out[t, 1, :, at] = acc[loc].astype(BF)
                i = order[loc]
                runs = [down_where[i * KB2 + k] for k in range(KB2)]
                lhs = jnp.concatenate([a[u // 8 * 16 + u % 8] for u in runs], axis=1)
                rhs = w2[pl.ds(i * KB2, KB2)].reshape(KB2 * BS, BS)
                out[t, 0, :, at] = jnp.dot(lhs, rhs, preferred_element_type=F32).astype(BF)


def down_terms_kernel(place, spot, where, a, g0, g1, f0, f1, out):
    z, q = place[0], place[1]

    def step(i, carry):
        at = spot[i]
        runs = [where[i * KB2 + k] for k in range(KB2)]
        lhs, rhs = [], []
        for tq, (g, f) in enumerate(((g0, f0), (g1, f1))):
            for tz in range(4):
                source = jnp.bitwise_xor(z, tz) * 2 + jnp.bitwise_xor(q, tq) + 8
                lhs.append(jnp.concatenate(
                    [a[u // 8 * 16 + source, pl.ds(pl.multiple_of(u % 8 * 16, 16), 16), :] for u in runs], axis=0
                ))
                rhs.append(block(g, at) if tz == 0 else f[at // 4, tz - 1, at // 2 % 2, :, lanes(at % 2)])
        got = jnp.dot(jnp.concatenate(lhs, axis=1), jnp.concatenate(rhs, axis=0), preferred_element_type=F32)
        out[pl.ds(i * KB2, KB2)] = got.reshape(KB2, 16, BS)
        return carry

    lax.fori_loop(0, ROWS, step, 0, unroll=2)


def close_kernel(got, out):
    out[...] = (got[0].astype(F32) + got[1].astype(F32)) + (got[2].astype(F32) + got[3].astype(F32))


def shift(value, axis, by):
    return lax.ppermute(value, axis, [(i, (i + by) % 4) for i in range(4)])


def swap(value, axis):
    return lax.ppermute(value, axis, [(0, 1), (1, 0)])


def across(value, by):
    return lax.ppermute(value, "z", [(i, i ^ by) for i in range(4)])


def after(value, *events):
    return lax.optimization_barrier((value, *events))[0]


def pieces(own, axis):
    return [own] + [shift(own, axis, -s) for s in (1, 2, 3)]


def exchange(parts, axis):
    return [parts[0]] + [shift(parts[s], axis, s) for s in (1, 2, 3)]


def total(parts):
    return sum((p.astype(F32) for p in parts[1:]), parts[0].astype(F32))


def local(inputs, grad_out, up_blocks, up_index, down_blocks, down_index):
    z, q, r, h, y = (lax.axis_index(a).astype(jnp.int32) for a in ("z", "q", "row", "h", "y"))
    place = jnp.stack([z, q])
    c = h * 4 + y

    def feature_spot(b):
        return ((b // 2 % 4 - y) % 4) * 4 + jnp.bitwise_xor(b // 8, h) * 2 + b % 2

    def feature_at(s):
        return jnp.bitwise_xor(s // 2 % 2, h) * 8 + ((s // 4 + y) % 4) * 2 + s % 2

    def hidden_spot(f):
        return ((f // 8 - r) % 4) * 8 + f % 8

    def hidden_at(s):
        return ((s // 8 + r) % 4) * 8 + s % 8

    features, units = jnp.arange(ROWS, dtype=jnp.int32), jnp.arange(COLS, dtype=jnp.int32)
    up_where = feature_spot(up_index - r * ROWS)
    down_where = hidden_spot(down_index - c * COLS)
    feature_spots, feature_order = feature_spot(features), feature_at(features)
    hidden_spots, hidden_order = hidden_spot(units), hidden_at(units)

    def shape(*dims, dtype=BF):
        return jax.ShapeDtypeStruct(dims, dtype)

    x_own = jnp.stack([inputs, swap(inputs, "h")])
    g_own = jnp.stack([grad_out, swap(grad_out, "h")])
    panel, piece = shape(8, BS, 2 * BS), shape(8, BS, BS)

    *parts, x, g = call(
        first_kernel, (hidden_order, feature_spots, up_where, down_where),
        (*pieces(x_own, "y"), *pieces(g_own, "y"), up_blocks, down_blocks),
        [shape(2, 8, BS, BS)] * 4 + [panel] * 2, [pltpu.VMEM((COLS, BS, BS), F32)], name="first",
    )
    parts = exchange(parts, "row")
    far1 = across(after(g_own, x), 1)
    far2 = across(jnp.stack([g_own, far1]), 2)
    x2, g2 = swap(x, "q"), swap(g, "q")
    (turned,) = call(turn_kernel, (place,), (x, x2), [shape(ROWS, 4, 16, 2 * BS)], name="turn")
    parts[0] = after(parts[0], turned, far2, g2)
    active, own, rows = call(act_kernel, (), parts, [piece, piece, shape(8, 8, 16, BS)], name="act")
    far = pieces(after(jnp.concatenate([far1[None], far2])[None], own), "y")
    rows = lax.all_to_all(rows, ("z", "q"), 0, 0, tiled=True)
    hidden = join(pieces(own, "row"))
    hidden2 = swap(after(hidden, rows, *far[1:]), "q")
    (terms,) = call(
        up_terms_kernel, (hidden_spots, up_where), (turned, hidden, hidden2), [shape(4, 128, 16, BS)], name="up_terms"
    )
    got = lax.all_to_all(terms, "z", 0, 0, tiled=True)
    both = jnp.concatenate([active, rows.reshape(8, BS, BS)])
    both = pieces(after(both, terms), "row")
    *ends, a = call(
        ends_kernel, (feature_order, hidden_spots, up_where, down_where), (hidden, *both, up_blocks, down_blocks),
        [shape(2, 2, BS, 2 * BS)] * 4 + [shape(64, BS, BS)], [pltpu.VMEM((ROWS, BS, BS), F32)], name="ends",
    )
    far[0] = after(far[0], *both[1:])
    far = join(far)
    (grad_down,) = call(
        down_terms_kernel, (place, feature_spots, down_where), (a, g, g2, far, swap(far, "q")),
        [shape(128, 16, BS, dtype=F32)], name="down_terms",
    )
    ends = exchange(ends, "y")
    ends[0] = after(ends[0], grad_down)
    mine = total(ends)
    ends = (mine[0] + swap(mine[1].astype(BF), "h").astype(F32)).astype(BF)
    (grad_up,) = call(close_kernel, (), (got,), [shape(128, 16, BS, dtype=F32)], name="close")
    return ends[0], ends[1], grad_up, grad_down


def solution(mesh):
    fine = Mesh(mesh.devices.reshape(4, 2, 4, 2, 4), ("z", "q", "row", "h", "y"))
    tokens, width = ("z", "q"), ("row", "h", "y")
    placed = (
        P(tokens, width),
        P(tokens, width),
        P(width, None, None),
        P(width),
        P(width, None, None),
        P(width),
    )
    return jax.shard_map(
        local,
        mesh=fine,
        in_specs=placed,
        out_specs=(P(tokens, width), P(tokens, width), P(width, tokens, None), P(width, tokens, None)),
        check_vma=False,
    )
```

```python
import jax
import jax.numpy as jnp
from jax import lax
from jax.experimental import pallas as pl
from jax.experimental.pallas import tpu as pltpu
from jax.sharding import Mesh
from jax.sharding import PartitionSpec as P

KB = 4
KB2 = 8
BS = 128
ROWS = 16
COLS = 32
BF = jnp.bfloat16
F32 = jnp.float32

gelu_scale = 0.7978845608028654
cubic_term = 0.044715


def gelu_both(values):
    tangent = jnp.tanh(gelu_scale * (values + cubic_term * values * values * values))
    value = 0.5 * values * (1.0 + tangent)
    slope = 0.5 * (1.0 + tangent) + 0.5 * values * (1.0 - tangent * tangent) * gelu_scale * (
        1.0 + 3.0 * cubic_term * values * values
    )
    return value, slope


SMEM = pl.BlockSpec(memory_space=pltpu.SMEM)
VMEM = pl.BlockSpec(memory_space=pltpu.VMEM)


def call(kernel, scalars, arrays, outs, scratch=(), name=None):
    return pl.pallas_call(
        kernel,
        out_shape=outs,
        in_specs=[SMEM] * len(scalars) + [VMEM] * len(arrays),
        out_specs=[VMEM] * len(outs),
        scratch_shapes=list(scratch),
        compiler_params=pltpu.CompilerParams(vmem_limit_bytes=28 * 2**20),
        cost_estimate=pl.CostEstimate(flops=1024, bytes_accessed=1024, transcendentals=0),
        name=name,
    )(*scalars, *arrays)


def lanes(half):
    return pl.ds(pl.multiple_of(half * BS, BS), BS)


def block(ref, at):
    return ref[at // 2, :, lanes(at % 2)]


def add_back(acc, run, where, width, rows, w):
    rhs = w[pl.ds(run * width, width)].reshape(width * BS, BS)
    got = lax.dot_general(rows, rhs, (((1,), (1,)), ((), ())), preferred_element_type=F32)
    for k in range(width):
        at = where[run * width + k]
        acc[at] = acc[at] + got[:, k * BS:(k + 1) * BS]


def first_kernel(order, spot, up_where, down_where, x0, x1, x2, x3, g0, g1, g2, g3, w1, w2, *rest):
    outs, x, g, acc = rest[:4], *rest[4:]
    for n, piece in enumerate((x0, x1, x2, x3)):
        x[n * 2:n * 2 + 2] = piece[...]
    for n, piece in enumerate((g0, g1, g2, g3)):
        g[n * 2:n * 2 + 2] = piece[...]
    acc[...] = jnp.zeros_like(acc)

    def back(i, carry):
        add_back(acc, i, down_where, KB2, block(g, spot[i]), w2)
        return carry

    lax.fori_loop(0, ROWS, back, 0, unroll=2)
    for slot, out in enumerate(outs):
        out[1] = acc[slot * 8:(slot + 1) * 8].astype(BF)

        def up(jj, carry):
            j = order[slot * 8 + jj]
            lhs = jnp.concatenate([block(x, up_where[j * KB + k]) for k in range(KB)], axis=1)
            rhs = w1[pl.ds(j * KB, KB)].reshape(KB * BS, BS)
            out[0, jj] = jnp.dot(lhs, rhs, preferred_element_type=F32).astype(BF)
            return carry

        lax.fori_loop(0, 8, up, 0, unroll=4)


def act_kernel(p0, p1, p2, p3, active, own, rows):
    def step(b, carry):
        hidden, grad = (
            p0[n, b].astype(F32) + p1[n, b].astype(F32) + p2[n, b].astype(F32) + p3[n, b].astype(F32) for n in range(2)
        )
        value, slope = gelu_both(hidden)
        own[b] = (grad * slope).astype(BF)
        value = value.astype(BF)
        active[b] = value
        turned = value.T.reshape(8, 16, BS)
        for d in range(8):
            rows[d, b] = turned[d]
        return carry

    lax.fori_loop(0, 8, step, 0, unroll=2)


def turn_kernel(place, x, x2, out):
    q = place[1]

    def step(p, carry):
        for half in range(2):
            for group, ref in enumerate((x, x2)):
                rows = ref[p, :, half * BS:(half + 1) * BS].T.reshape(4, 2, 16, BS)
                for zz in range(4):
                    mine = jnp.where(q == 0, rows[zz, 0], rows[zz, 1])
                    out[p * 2 + half, zz, :, group * BS:(group + 1) * BS] = mine
        return carry

    lax.fori_loop(0, 8, step, 0, unroll=2)


def join_kernel(p0, p1, p2, p3, out):
    size = p0.shape[0]
    for n, piece in enumerate((p0, p1, p2, p3)):
        out[n * size:(n + 1) * size] = piece[...]


def join(parts):
    first = parts[0]
    whole = jax.ShapeDtypeStruct((4 * first.shape[0], *first.shape[1:]), first.dtype)
    return call(join_kernel, (), parts, [whole], name="join")[0]


def up_terms_kernel(spot, where, xt, v0, v1, out):
    def step(j, carry):
        at = spot[j]
        lhs = jnp.concatenate([xt[where[j * KB + k]].reshape(64, 2 * BS) for k in range(KB)], axis=0)
        rhs = jnp.concatenate([v0[at], v1[at]], axis=0)
        got = jnp.dot(lhs, rhs, preferred_element_type=F32).astype(BF).reshape(KB, 4, 16, BS)
        for zz in range(4):
            out[zz, pl.ds(j * KB, KB)] = got[:, zz]
        return carry

    lax.fori_loop(0, COLS, step, 0, unroll=2)


def ends_kernel(order, spot, up_where, down_where, v, a0, a1, a2, a3, w1, w2, o0, o1, o2, o3, a, acc):
    for n, piece in enumerate((a0, a1, a2, a3)):
        a[n * 16:n * 16 + 16] = piece[...]
    acc[...] = jnp.zeros_like(acc)

    def step(j, carry):
        add_back(acc, j, up_where, KB, v[spot[j]], w1)
        return carry

    lax.fori_loop(0, COLS, step, 0, unroll=4)
    for slot, out in enumerate((o0, o1, o2, o3)):
        for t in range(2):
            for half in range(2):
                loc = slot * 4 + t * 2 + half
                at = slice(half * BS, (half + 1) * BS)
                out[t, 1, :, at] = acc[loc].astype(BF)
                i = order[loc]
                runs = [down_where[i * KB2 + k] for k in range(KB2)]
                lhs = jnp.concatenate([a[u // 8 * 16 + u % 8] for u in runs], axis=1)
                rhs = w2[pl.ds(i * KB2, KB2)].reshape(KB2 * BS, BS)
                out[t, 0, :, at] = jnp.dot(lhs, rhs, preferred_element_type=F32).astype(BF)


def down_terms_kernel(place, spot, where, a, g0, g1, f0, f1, out):
    z, q = place[0], place[1]

    def step(i, carry):
        at = spot[i]
        runs = [where[i * KB2 + k] for k in range(KB2)]
        lhs, rhs = [], []
        for tq, (g, f) in enumerate(((g0, f0), (g1, f1))):
            for tz in range(4):
                source = jnp.bitwise_xor(z, tz) * 2 + jnp.bitwise_xor(q, tq) + 8
                lhs.append(jnp.concatenate(
                    [a[u // 8 * 16 + source, pl.ds(pl.multiple_of(u % 8 * 16, 16), 16), :] for u in runs], axis=0
                ))
                rhs.append(block(g, at) if tz == 0 else f[at // 4, tz - 1, at // 2 % 2, :, lanes(at % 2)])
        got = jnp.dot(jnp.concatenate(lhs, axis=1), jnp.concatenate(rhs, axis=0), preferred_element_type=F32)
        out[pl.ds(i * KB2, KB2)] = got.reshape(KB2, 16, BS)
        return carry

    lax.fori_loop(0, ROWS, step, 0, unroll=2)


def close_kernel(got, out):
    out[...] = (got[0].astype(F32) + got[1].astype(F32)) + (got[2].astype(F32) + got[3].astype(F32))


def shift(value, axis, by):
    return lax.ppermute(value, axis, [(i, (i + by) % 4) for i in range(4)])


def swap(value, axis):
    return lax.ppermute(value, axis, [(0, 1), (1, 0)])


def across(value, by):
    return lax.ppermute(value, "z", [(i, i ^ by) for i in range(4)])


def after(value, *events):
    return lax.optimization_barrier((value, *events))[0]


def pieces(own, axis):
    return [own] + [shift(own, axis, -s) for s in (1, 2, 3)]


def exchange(parts, axis):
    return [parts[0]] + [shift(parts[s], axis, s) for s in (1, 2, 3)]


def total(parts):
    return sum((p.astype(F32) for p in parts[1:]), parts[0].astype(F32))


def local(inputs, grad_out, up_blocks, up_index, down_blocks, down_index):
    z, q, r, h, y = (lax.axis_index(a).astype(jnp.int32) for a in ("z", "q", "row", "h", "y"))
    place = jnp.stack([z, q])
    c = h * 4 + y

    def feature_spot(b):
        return ((b // 2 % 4 - y) % 4) * 4 + jnp.bitwise_xor(b // 8, h) * 2 + b % 2

    def feature_at(s):
        return jnp.bitwise_xor(s // 2 % 2, h) * 8 + ((s // 4 + y) % 4) * 2 + s % 2

    def hidden_spot(f):
        return ((f // 8 - r) % 4) * 8 + f % 8

    def hidden_at(s):
        return ((s // 8 + r) % 4) * 8 + s % 8

    features, units = jnp.arange(ROWS, dtype=jnp.int32), jnp.arange(COLS, dtype=jnp.int32)
    up_where = feature_spot(up_index - r * ROWS)
    down_where = hidden_spot(down_index - c * COLS)
    feature_spots, feature_order = feature_spot(features), feature_at(features)
    hidden_spots, hidden_order = hidden_spot(units), hidden_at(units)

    def shape(*dims, dtype=BF):
        return jax.ShapeDtypeStruct(dims, dtype)

    x_own = jnp.stack([inputs, swap(inputs, "h")])
    g_own = jnp.stack([grad_out, swap(grad_out, "h")])
    panel, piece = shape(8, BS, 2 * BS), shape(8, BS, BS)

    *parts, x, g = call(
        first_kernel, (hidden_order, feature_spots, up_where, down_where),
        (*pieces(x_own, "y"), *pieces(g_own, "y"), up_blocks, down_blocks),
        [shape(2, 8, BS, BS)] * 4 + [panel] * 2, [pltpu.VMEM((COLS, BS, BS), F32)], name="first",
    )
    parts = exchange(parts, "row")
    far1 = across(after(g_own, x), 1)
    far2 = across(jnp.stack([g_own, far1]), 2)
    x2, g2 = swap(x, "q"), swap(g, "q")
    (turned,) = call(turn_kernel, (place,), (x, x2), [shape(ROWS, 4, 16, 2 * BS)], name="turn")
    parts[0] = after(parts[0], turned, far2, g2)
    active, own, rows = call(act_kernel, (), parts, [piece, piece, shape(8, 8, 16, BS)], name="act")
    far = pieces(after(jnp.concatenate([far1[None], far2])[None], own), "y")
    rows = lax.all_to_all(rows, ("z", "q"), 0, 0, tiled=True)
    hidden = join(pieces(own, "row"))
    hidden2 = swap(after(hidden, rows, *far[1:]), "q")
    (terms,) = call(
        up_terms_kernel, (hidden_spots, up_where), (turned, hidden, hidden2), [shape(4, 128, 16, BS)], name="up_terms"
    )
    got = lax.all_to_all(terms, "z", 0, 0, tiled=True)
    both = jnp.concatenate([active, rows.reshape(8, BS, BS)])
    both = pieces(after(both, hidden), "row")
    *ends, a = call(
        ends_kernel, (feature_order, hidden_spots, up_where, down_where), (hidden, *both, up_blocks, down_blocks),
        [shape(2, 2, BS, 2 * BS)] * 4 + [shape(64, BS, BS)], [pltpu.VMEM((ROWS, BS, BS), F32)], name="ends",
    )
    far[0] = after(far[0], a)
    far = join(far)
    (grad_down,) = call(
        down_terms_kernel, (place, feature_spots, down_where), (a, g, g2, far, swap(far, "q")),
        [shape(128, 16, BS, dtype=F32)], name="down_terms",
    )
    ends = exchange(ends, "y")
    ends[0] = after(ends[0], grad_down)
    mine = total(ends)
    ends = (mine[0] + swap(mine[1].astype(BF), "h").astype(F32)).astype(BF)
    (grad_up,) = call(close_kernel, (), (got,), [shape(128, 16, BS, dtype=F32)], name="close")
    return ends[0], ends[1], grad_up, grad_down


def solution(mesh):
    fine = Mesh(mesh.devices.reshape(4, 2, 4, 2, 4), ("z", "q", "row", "h", "y"))
    tokens, width = ("z", "q"), ("row", "h", "y")
    placed = (
        P(tokens, width),
        P(tokens, width),
        P(width, None, None),
        P(width),
        P(width, None, None),
        P(width),
    )
    return jax.shard_map(
        local,
        mesh=fine,
        in_specs=placed,
        out_specs=(P(tokens, width), P(tokens, width), P(width, tokens, None), P(width, tokens, None)),
        check_vma=False,
    )
```

```python
import jax
import jax.numpy as jnp
from jax import lax
from jax.experimental import pallas as pl
from jax.experimental.pallas import tpu as pltpu
from jax.sharding import Mesh
from jax.sharding import PartitionSpec as P

KB = 4
KB2 = 8
BS = 128
ROWS = 16
COLS = 32
BF = jnp.bfloat16
F32 = jnp.float32

gelu_scale = 0.7978845608028654
cubic_term = 0.044715


def gelu_both(values):
    tangent = jnp.tanh(gelu_scale * (values + cubic_term * values * values * values))
    value = 0.5 * values * (1.0 + tangent)
    slope = 0.5 * (1.0 + tangent) + 0.5 * values * (1.0 - tangent * tangent) * gelu_scale * (
        1.0 + 3.0 * cubic_term * values * values
    )
    return value, slope


SMEM = pl.BlockSpec(memory_space=pltpu.SMEM)
VMEM = pl.BlockSpec(memory_space=pltpu.VMEM)


def call(kernel, scalars, arrays, outs, scratch=(), name=None):
    return pl.pallas_call(
        kernel,
        out_shape=outs,
        in_specs=[SMEM] * len(scalars) + [VMEM] * len(arrays),
        out_specs=[VMEM] * len(outs),
        scratch_shapes=list(scratch),
        compiler_params=pltpu.CompilerParams(vmem_limit_bytes=28 * 2**20),
        cost_estimate=pl.CostEstimate(flops=1024, bytes_accessed=1024, transcendentals=0),
        name=name,
    )(*scalars, *arrays)


def lanes(half):
    return pl.ds(pl.multiple_of(half * BS, BS), BS)


def block(ref, at):
    return ref[at // 2, :, lanes(at % 2)]


def add_back(acc, run, where, width, rows, w):
    rhs = w[pl.ds(run * width, width)].reshape(width * BS, BS)
    got = lax.dot_general(rows, rhs, (((1,), (1,)), ((), ())), preferred_element_type=F32)
    for k in range(width):
        at = where[run * width + k]
        acc[at] = acc[at] + got[:, k * BS:(k + 1) * BS]


def first_kernel(order, spot, up_where, down_where, x0, x1, x2, x3, g0, g1, g2, g3, w1, w2, *rest):
    outs, x, g, acc = rest[:4], *rest[4:]
    for n, piece in enumerate((x0, x1, x2, x3)):
        x[n * 2:n * 2 + 2] = piece[...]
    for n, piece in enumerate((g0, g1, g2, g3)):
        g[n * 2:n * 2 + 2] = piece[...]
    acc[...] = jnp.zeros_like(acc)

    def back(i, carry):
        add_back(acc, i, down_where, KB2, block(g, spot[i]), w2)
        return carry

    lax.fori_loop(0, ROWS, back, 0, unroll=2)
    for slot, out in enumerate(outs):
        out[1] = acc[slot * 8:(slot + 1) * 8].astype(BF)

        def up(jj, carry):
            j = order[slot * 8 + jj]
            lhs = jnp.concatenate([block(x, up_where[j * KB + k]) for k in range(KB)], axis=1)
            rhs = w1[pl.ds(j * KB, KB)].reshape(KB * BS, BS)
            out[0, jj] = jnp.dot(lhs, rhs, preferred_element_type=F32).astype(BF)
            return carry

        lax.fori_loop(0, 8, up, 0, unroll=4)


def act_kernel(p0, p1, p2, p3, active, own, rows):
    def step(b, carry):
        hidden, grad = (
            p0[n, b].astype(F32) + p1[n, b].astype(F32) + p2[n, b].astype(F32) + p3[n, b].astype(F32) for n in range(2)
        )
        value, slope = gelu_both(hidden)
        own[b] = (grad * slope).astype(BF)
        value = value.astype(BF)
        active[b] = value
        turned = value.T.reshape(8, 16, BS)
        for d in range(8):
            rows[d, b] = turned[d]
        return carry

    lax.fori_loop(0, 8, step, 0, unroll=2)


def turn_kernel(place, x, x2, out):
    q = place[1]

    def step(p, carry):
        for half in range(2):
            for group, ref in enumerate((x, x2)):
                rows = ref[p, :, half * BS:(half + 1) * BS].T.reshape(4, 2, 16, BS)
                for zz in range(4):
                    mine = jnp.where(q == 0, rows[zz, 0], rows[zz, 1])
                    out[p * 2 + half, zz, :, group * BS:(group + 1) * BS] = mine
        return carry

    lax.fori_loop(0, 8, step, 0, unroll=2)


def join_kernel(p0, p1, p2, p3, out):
    size = p0.shape[0]
    for n, piece in enumerate((p0, p1, p2, p3)):
        out[n * size:(n + 1) * size] = piece[...]


def join(parts):
    first = parts[0]
    whole = jax.ShapeDtypeStruct((4 * first.shape[0], *first.shape[1:]), first.dtype)
    return call(join_kernel, (), parts, [whole], name="join")[0]


def up_terms_kernel(spot, where, xt, v0, v1, out):
    def step(j, carry):
        at = spot[j]
        lhs = jnp.concatenate([xt[where[j * KB + k]].reshape(64, 2 * BS) for k in range(KB)], axis=0)
        rhs = jnp.concatenate([v0[at], v1[at]], axis=0)
        got = jnp.dot(lhs, rhs, preferred_element_type=F32).astype(BF).reshape(KB, 4, 16, BS)
        for zz in range(4):
            out[zz, pl.ds(j * KB, KB)] = got[:, zz]
        return carry

    lax.fori_loop(0, COLS, step, 0, unroll=2)


def ends_kernel(order, spot, up_where, down_where, v, a0, a1, a2, a3, w1, w2, o0, o1, o2, o3, a, acc):
    for n, piece in enumerate((a0, a1, a2, a3)):
        a[n * 16:n * 16 + 16] = piece[...]
    acc[...] = jnp.zeros_like(acc)

    def step(j, carry):
        add_back(acc, j, up_where, KB, v[spot[j]], w1)
        return carry

    lax.fori_loop(0, COLS, step, 0, unroll=4)
    for slot, out in enumerate((o0, o1, o2, o3)):
        for t in range(2):
            for half in range(2):
                loc = slot * 4 + t * 2 + half
                at = slice(half * BS, (half + 1) * BS)
                out[t, 1, :, at] = acc[loc].astype(BF)
                i = order[loc]
                runs = [down_where[i * KB2 + k] for k in range(KB2)]
                lhs = jnp.concatenate([a[u // 8 * 16 + u % 8] for u in runs], axis=1)
                rhs = w2[pl.ds(i * KB2, KB2)].reshape(KB2 * BS, BS)
                out[t, 0, :, at] = jnp.dot(lhs, rhs, preferred_element_type=F32).astype(BF)


def down_terms_kernel(place, spot, where, a, g0, g1, f0, f1, out):
    z, q = place[0], place[1]

    def step(i, carry):
        at = spot[i]
        runs = [where[i * KB2 + k] for k in range(KB2)]
        lhs, rhs = [], []
        for tq, (g, f) in enumerate(((g0, f0), (g1, f1))):
            for tz in range(4):
                source = jnp.bitwise_xor(z, tz) * 2 + jnp.bitwise_xor(q, tq) + 8
                lhs.append(jnp.concatenate(
                    [a[u // 8 * 16 + source, pl.ds(pl.multiple_of(u % 8 * 16, 16), 16), :] for u in runs], axis=0
                ))
                rhs.append(block(g, at) if tz == 0 else f[at // 4, tz - 1, at // 2 % 2, :, lanes(at % 2)])
        got = jnp.dot(jnp.concatenate(lhs, axis=1), jnp.concatenate(rhs, axis=0), preferred_element_type=F32)
        out[pl.ds(i * KB2, KB2)] = got.reshape(KB2, 16, BS)
        return carry

    lax.fori_loop(0, ROWS, step, 0, unroll=2)


def close_kernel(got, out):
    out[...] = (got[0].astype(F32) + got[1].astype(F32)) + (got[2].astype(F32) + got[3].astype(F32))


def shift(value, axis, by):
    return lax.ppermute(value, axis, [(i, (i + by) % 4) for i in range(4)])


def swap(value, axis):
    return lax.ppermute(value, axis, [(0, 1), (1, 0)])


def across(value, by):
    return lax.ppermute(value, "z", [(i, i ^ by) for i in range(4)])


def after(value, *events):
    return lax.optimization_barrier((value, *events))[0]


def pieces(own, axis):
    return [own] + [shift(own, axis, -s) for s in (1, 2, 3)]


def exchange(parts, axis):
    return [parts[0]] + [shift(parts[s], axis, s) for s in (1, 2, 3)]


def total(parts):
    return sum((p.astype(F32) for p in parts[1:]), parts[0].astype(F32))


def local(inputs, grad_out, up_blocks, up_index, down_blocks, down_index):
    z, q, r, h, y = (lax.axis_index(a).astype(jnp.int32) for a in ("z", "q", "row", "h", "y"))
    place = jnp.stack([z, q])
    c = h * 4 + y

    def feature_spot(b):
        return ((b // 2 % 4 - y) % 4) * 4 + jnp.bitwise_xor(b // 8, h) * 2 + b % 2

    def feature_at(s):
        return jnp.bitwise_xor(s // 2 % 2, h) * 8 + ((s // 4 + y) % 4) * 2 + s % 2

    def hidden_spot(f):
        return ((f // 8 - r) % 4) * 8 + f % 8

    def hidden_at(s):
        return ((s // 8 + r) % 4) * 8 + s % 8

    features, units = jnp.arange(ROWS, dtype=jnp.int32), jnp.arange(COLS, dtype=jnp.int32)
    up_where = feature_spot(up_index - r * ROWS)
    down_where = hidden_spot(down_index - c * COLS)
    feature_spots, feature_order = feature_spot(features), feature_at(features)
    hidden_spots, hidden_order = hidden_spot(units), hidden_at(units)

    def shape(*dims, dtype=BF):
        return jax.ShapeDtypeStruct(dims, dtype)

    x_own = jnp.stack([inputs, swap(inputs, "h")])
    g_own = jnp.stack([grad_out, swap(grad_out, "h")])
    panel, piece = shape(8, BS, 2 * BS), shape(8, BS, BS)

    *parts, x, g = call(
        first_kernel, (hidden_order, feature_spots, up_where, down_where),
        (*pieces(x_own, "y"), *pieces(g_own, "y"), up_blocks, down_blocks),
        [shape(2, 8, BS, BS)] * 4 + [panel] * 2, [pltpu.VMEM((COLS, BS, BS), F32)], name="first",
    )
    parts = exchange(parts, "row")
    far1 = across(after(g_own, x), 1)
    far2 = across(jnp.stack([g_own, far1]), 2)
    x2, g2 = swap(x, "q"), swap(g, "q")
    (turned,) = call(turn_kernel, (place,), (x, x2), [shape(ROWS, 4, 16, 2 * BS)], name="turn")
    parts[0] = after(parts[0], turned, far2, g2)
    active, own, rows = call(act_kernel, (), parts, [piece, piece, shape(8, 8, 16, BS)], name="act")
    rows = lax.all_to_all(rows, ("z", "q"), 0, 0, tiled=True)
    hidden = pieces(own, "row")
    hidden[0] = after(hidden[0], rows)
    hidden = join(hidden)
    far = pieces(after(jnp.concatenate([far1[None], far2])[None], hidden), "y")
    hidden2 = swap(hidden, "q")
    (terms,) = call(
        up_terms_kernel, (hidden_spots, up_where), (turned, hidden, hidden2), [shape(4, 128, 16, BS)], name="up_terms"
    )
    got = lax.all_to_all(terms, "z", 0, 0, tiled=True)
    both = jnp.concatenate([active, rows.reshape(8, BS, BS)])
    both = pieces(after(both, hidden), "row")
    *ends, a = call(
        ends_kernel, (feature_order, hidden_spots, up_where, down_where), (hidden, *both, up_blocks, down_blocks),
        [shape(2, 2, BS, 2 * BS)] * 4 + [shape(64, BS, BS)], [pltpu.VMEM((ROWS, BS, BS), F32)], name="ends",
    )
    far[0] = after(far[0], a)
    far = join(far)
    (grad_down,) = call(
        down_terms_kernel, (place, feature_spots, down_where), (a, g, g2, far, swap(far, "q")),
        [shape(128, 16, BS, dtype=F32)], name="down_terms",
    )
    ends = exchange(ends, "y")
    ends[0] = after(ends[0], grad_down)
    mine = total(ends)
    ends = (mine[0] + swap(mine[1].astype(BF), "h").astype(F32)).astype(BF)
    (grad_up,) = call(close_kernel, (), (got,), [shape(128, 16, BS, dtype=F32)], name="close")
    return ends[0], ends[1], grad_up, grad_down


def solution(mesh):
    fine = Mesh(mesh.devices.reshape(4, 2, 4, 2, 4), ("z", "q", "row", "h", "y"))
    tokens, width = ("z", "q"), ("row", "h", "y")
    placed = (
        P(tokens, width),
        P(tokens, width),
        P(width, None, None),
        P(width),
        P(width, None, None),
        P(width),
    )
    return jax.shard_map(
        local,
        mesh=fine,
        in_specs=placed,
        out_specs=(P(tokens, width), P(tokens, width), P(width, tokens, None), P(width, tokens, None)),
        check_vma=False,
    )
```
